256 devices in a mesh: lon: 32 (over x_lo, z, core), lat: 8 (over x_hi, y).
Axes of the slice: x: 4 (x_hi: 2, x_lo: 2; x = x_hi * 2 + x_lo), y: 4, z: 8, core: 2. Of those that a mesh axis runs over, the one named last changes fastest.
Arguments:
- tokens: bfloat16 [4, 48, 384, 512], P(None, 'lat', 'lon'), may hold values from -45 to 45
- gain_attn: float32 [512], replicated, may hold values from 0.1 to 1.9
- w_qkv: bfloat16 [512, 1536], replicated, may hold values from -8 to 8
- w_out: bfloat16 [512, 512], replicated, may hold values from -0.25 to 0.25
- gain_mlp: float32 [512], replicated, may hold values from 0.1 to 1.9
- w_up: bfloat16 [512, 2048], replicated, may hold values from -0.25 to 0.25
- w_down: bfloat16 [2048, 512], replicated, may hold values from -0.125 to 0.125
Outputs:
- block_out: bfloat16 [4, 48, 384, 512], P(None, 'lat', 'lon')
The draws below stay inside these ranges and needn't reach their ends.
All inputs are finite; a program needn't handle non-finite values.
Results may differ from the reference program's by a relative error of at most 0.014.
The reference program's roundings to bfloat16 on the way (of `normed`, `qkv`, `weights`, `attended`, `residual`, `normed_mlp` and `hidden`) count: a program that leaves them out, or rounds other values in their place, can miss the bound.
Values may be sent and summed in bfloat16 or wider, within the bound.
A program may use at most 128 MiB of HBM per device.

```python
import jax
import jax.numpy as jnp
from jax import lax

D = 512
HEADS = 8
FF_WIDTH = 2048
LEVELS = 4
NLAT = 48
NLON = 384


def draw_tokens(key, part):
    key = jax.random.fold_in(key, 11)
    first, second, third = jax.random.split(key, 3)
    col_scale = jnp.exp(jax.random.uniform(second, (D,), jnp.float32, -1.15, 1.15))
    row_scale = jnp.exp(jax.random.uniform(third, (LEVELS, NLAT, NLON, 1), jnp.float32, -1.15, 1.15))
    base = jnp.clip(jax.random.normal(first, (LEVELS, NLAT, NLON, D), jnp.float32), -4.0, 4.0)
    values = base * col_scale * row_scale
    return values.astype(jnp.bfloat16)


def draw_w_qkv(key, part):
    key = jax.random.fold_in(key, 23)
    values = jnp.clip(jax.random.normal(key, (D, 3 * D), jnp.float32), -4.0, 4.0) * D ** (-0.5)
    return values.astype(jnp.bfloat16)


def gaussian(rng, dims, scale, bound, dtype=jnp.bfloat16):
    return jnp.clip(scale * jax.random.normal(rng, dims, jnp.float32), -bound, bound).astype(dtype)


def setup_inputs(seed: int = 0) -> dict:
    seeds = jax.random.split(jax.random.key(seed), 8)
    tokens = draw_tokens(jax.random.fold_in(seeds[7], 71), 0)
    gain_attn = jnp.clip(1.0 + 0.18 * jax.random.normal(seeds[1], (D,), jnp.float32), 0.1, 1.9)
    w_qkv = draw_w_qkv(jax.random.fold_in(seeds[7], 71), 0)
    w_out = gaussian(seeds[3], (D, D), D ** -0.5, 0.25)
    gain_mlp = jnp.clip(1.0 + 0.18 * jax.random.normal(seeds[4], (D,), jnp.float32), 0.1, 1.9)
    w_up = gaussian(seeds[5], (D, FF_WIDTH), D ** -0.5, 0.25)
    w_down = gaussian(seeds[6], (FF_WIDTH, D), FF_WIDTH ** -0.5, 0.125)
    return dict(tokens=tokens, gain_attn=gain_attn, w_qkv=w_qkv, w_out=w_out, gain_mlp=gain_mlp, w_up=w_up, w_down=w_down)


def layer_norm(values, gain_vec):
    values = values.astype(jnp.float32)
    average = lax.optimization_barrier(jnp.mean(values, axis=-1, keepdims=True))
    centered = values - average
    spread = lax.optimization_barrier(jnp.mean(centered * centered, axis=-1, keepdims=True))
    return centered * lax.rsqrt(spread + 1e-05) * gain_vec

def split_windows(tile_block):
    levels, lat_rows, lon_cols, features = tile_block.shape
    parted = tile_block.reshape(levels // 2, 2, lat_rows // 6, 6, lon_cols // 12, 12, features)
    parted = parted.transpose(0, 2, 4, 1, 3, 5, 6)
    return parted.reshape(-1, 144, features)

def merge_windows(parted, levels, lat_rows, lon_cols):
    features = parted.shape[-1]
    tile_block = parted.reshape(levels // 2, lat_rows // 6, lon_cols // 12, 2, 6, 12, features)
    tile_block = tile_block.transpose(0, 3, 1, 4, 2, 5, 6)
    return tile_block.reshape(levels, lat_rows, lon_cols, features)

def token_keys(key_table, lon_cols):
    levels, lat_rows = key_table.shape
    widened = jnp.broadcast_to(key_table[:, :, None, None], (levels, lat_rows, lon_cols, 1))
    return split_windows(widened)[..., 0]

def attend(queries, keyval, level_table, row_table, usable, num_heads):
    levels, lat_rows, lon_cols, features = queries.shape
    head_dim = features // num_heads
    query_win = split_windows(queries)
    keyval_win = split_windows(keyval)
    windows = query_win.shape[0]
    allowed = None
    for key_table in (level_table, row_table):
        window_key = token_keys(key_table, lon_cols)
        agrees = window_key[:, :, None] == window_key[:, None, :]
        allowed = agrees if allowed is None else allowed & agrees
    allowed = allowed & (token_keys(usable, lon_cols)[:, None, :] > 0.5)
    query_heads = query_win.reshape(windows, 144, num_heads, head_dim).astype(jnp.float32)
    key_heads = keyval_win[..., :features].reshape(windows, 144, num_heads, head_dim).astype(jnp.float32)
    value_heads = keyval_win[..., features:].reshape(windows, 144, num_heads, head_dim).astype(jnp.float32)
    scores = jnp.einsum('wqhd,wkhd->whqk', query_heads, key_heads) * head_dim ** (-0.5)
    scores = jnp.where(allowed[:, None], scores, -1e+30)
    ceiling = lax.optimization_barrier(jnp.max(scores, axis=-1, keepdims=True))
    raised = jnp.exp(scores - ceiling)
    weights = (raised / lax.optimization_barrier(jnp.sum(raised, axis=-1, keepdims=True))).astype(jnp.bfloat16)
    attended = jnp.einsum('whqk,wkhd->wqhd', weights.astype(jnp.float32), value_heads).astype(jnp.bfloat16)
    return merge_windows(attended.reshape(windows, 144, features), levels, lat_rows, lon_cols)

def reference(tokens, gain_attn, w_qkv, w_out, gain_mlp, w_up, w_down):
    levels, total_rows, total_cols, features = tokens.shape
    groups = total_cols // 12
    rolled = jnp.roll(tokens, (-1, -3, -6), axis=(0, 1, 2))
    level_order = (jnp.arange(levels) + 1) % levels
    level_table = jnp.broadcast_to(((level_order + 1) // 2).astype(jnp.float32)[:, None], (levels, total_rows))
    row_order = (jnp.arange(total_rows) + 3) % total_rows
    row_table = jnp.broadcast_to(((row_order + 3) // 6).astype(jnp.float32)[None, :], (levels, total_rows))
    usable = jnp.ones((levels, total_rows), jnp.float32)
    tiles = jnp.moveaxis(rolled.reshape(levels, total_rows, groups, 12, features), 2, 0)

    def window_group(tile_block):
        normed = layer_norm(tile_block, gain_attn).astype(jnp.bfloat16)
        qkv = jnp.dot(normed.reshape(-1, features), w_qkv, preferred_element_type=jnp.float32).astype(jnp.bfloat16)
        qkv = qkv.reshape(levels, total_rows, 12, 3 * features)
        return attend(qkv[..., :features], qkv[..., features:], level_table, row_table, usable, HEADS)
    attended = lax.map(window_group, tiles)
    attended = jnp.moveaxis(attended, 0, 2).reshape(levels, total_rows, total_cols, features)
    attended = jnp.roll(attended, (1, 3, 6), axis=(0, 1, 2))

    def feed_forward(paired):
        source, mixed_in = paired
        mixed = jnp.dot(mixed_in.reshape(-1, features), w_out, preferred_element_type=jnp.float32)
        residual = (source.reshape(-1, features).astype(jnp.float32) + mixed).astype(jnp.bfloat16)
        normed_mlp = layer_norm(residual, gain_mlp).astype(jnp.bfloat16)
        hidden = jax.nn.gelu(jnp.dot(normed_mlp, w_up, preferred_element_type=jnp.float32)).astype(jnp.bfloat16)
        block_out = residual.astype(jnp.float32) + jnp.dot(hidden, w_down, preferred_element_type=jnp.float32)
        return block_out.astype(jnp.bfloat16).reshape(source.shape)
    source_tiles = jnp.moveaxis(tokens.reshape(levels, total_rows, groups, 12, features), 2, 0)
    mixed_tiles = jnp.moveaxis(attended.reshape(levels, total_rows, groups, 12, features), 2, 0)
    outputs = lax.map(feed_forward, (source_tiles, mixed_tiles))
    return jnp.moveaxis(outputs, 0, 2).reshape(tokens.shape)
```

```python
import functools

import jax
import jax.numpy as jnp
from jax import lax
from jax.experimental import pallas as pl
from jax.experimental.pallas import tpu as pltpu
from jax.sharding import PartitionSpec as P

HEADS = 8
D = 512
FF = 2048
HEAD_DIM = 64
F32 = jnp.float32
BF16 = jnp.bfloat16
MESH = pl.DeviceIdType.MESH


def norm(values, gain):
    average = jnp.mean(values, axis=-1, keepdims=True)
    centered = values - average
    spread = jnp.mean(centered * centered, axis=-1, keepdims=True)
    return (centered * lax.rsqrt(spread + 1e-05) * gain).astype(BF16)


def flat(block):
    rows = block.shape[0] * block.shape[1] * block.shape[2]
    return block.reshape(rows, block.shape[3])


def gelu(v):
    inner = v * (0.7978845608028654 + 0.035677408136300125 * (v * v))
    return (0.5 * v) * (1.0 + jnp.tanh(inner))


def dot(a, b):
    return jnp.dot(a, b, preferred_element_type=F32)


def dot_t(a, b):
    return lax.dot_general(a, b, (((1,), (1,)), ((), ())), preferred_element_type=F32)


def kernel(
    n_lat,
    n_lon,
    x_hbm,
    gain_attn,
    w_qkv_hbm,
    w_out_hbm,
    gain_mlp,
    w_up_hbm,
    w_down_hbm,
    o_ref,
    xv,
    halo,
    back,
    got,
    bias,
    w_qkv,
    w_out,
    w_up,
    w_down,
    send_sem,
    recv_sem,
    back_send,
    back_recv,
    w_sem,
    x_sem,
):
    lat = lax.axis_index("lat")
    lon = lax.axis_index("lon")
    west = lax.rem(lon + n_lon - 1, n_lon)
    east = lax.rem(lon + 1, n_lon)
    has_north = lat > 0
    has_south = lat < n_lat - 1

    barrier = pltpu.get_barrier_semaphore()

    def greet(la, lo):
        pl.semaphore_signal(barrier, inc=1, device_id={"lat": la, "lon": lo}, device_id_type=MESH)

    greet(lat, west)

    @pl.when(has_north)
    def _():
        greet(lat - 1, lon)
        greet(lat - 1, west)

    @pl.when(has_south)
    def _():
        greet(lat + 1, lon)
        greet(lat + 1, west)

    loads = [
        pltpu.make_async_copy(x_hbm, xv, x_sem.at[0]),
        pltpu.make_async_copy(x_hbm.at[:, 0:6], halo.at[3:9, 6:12], x_sem.at[1]),
        pltpu.make_async_copy(w_qkv_hbm, w_qkv, w_sem.at[0]),
        pltpu.make_async_copy(w_out_hbm, w_out, w_sem.at[1]),
        pltpu.make_async_copy(w_up_hbm, w_up, w_sem.at[2]),
        pltpu.make_async_copy(w_down_hbm, w_down, w_sem.at[3]),
    ]
    for load in loads:
        load.start()

    def send(index, src, dst, la, lo):
        return pltpu.make_async_remote_copy(
            src_ref=src,
            dst_ref=dst,
            send_sem=send_sem.at[index],
            recv_sem=recv_sem.at[index],
            device_id={"lat": la, "lon": lo},
            device_id_type=MESH,
        )

    to_east = send(0, x_hbm.at[:, 6:12], halo.at[3:9, 0:6], lat, east)
    to_north = [
        send(1, x_hbm.at[0:3, 0:6], halo.at[9:12, 6:12], lat - 1, lon),
        send(2, x_hbm.at[0:3, 6:12], halo.at[9:12, 0:6], lat - 1, east),
    ]
    to_south = [
        send(3, x_hbm.at[3:6, 0:6], halo.at[0:3, 6:12], lat + 1, lon),
        send(4, x_hbm.at[3:6, 6:12], halo.at[0:3, 0:6], lat + 1, east),
    ]

    pl.semaphore_wait(barrier, 1 + 2 * (has_north.astype(jnp.int32) + has_south.astype(jnp.int32)))
    to_east.start()

    @pl.when(has_north)
    def _():
        for copy in to_north:
            copy.start()

    @pl.when(has_south)
    def _():
        for copy in to_south:
            copy.start()

    key = lax.broadcasted_iota(jnp.int32, (144, 288), 1)
    query = lax.broadcasted_iota(jnp.int32, (144, 288), 0)
    same = lax.div(lax.rem(key, 4) + 1, 2) == lax.div(lax.rem(query, 4) + 1, 2)
    bias[0] = jnp.where(same & ((key >= 144) | has_north), 0.0, -1e30)
    bias[1] = jnp.where(same & ((key < 144) | has_south), 0.0, -1e30)

    @pl.when(jnp.logical_not(has_north))
    def _():
        halo[0:3] = jnp.zeros((3, 12, 4, D), BF16)

    @pl.when(jnp.logical_not(has_south))
    def _():
        halo[9:12] = jnp.zeros((3, 12, 4, D), BF16)

    loads[0].wait()
    loads[1].wait()
    loads[2].wait()
    to_east.wait_recv()

    def give_back(band):
        return pltpu.make_async_remote_copy(
            src_ref=back.at[band],
            dst_ref=got.at[band],
            send_sem=back_send.at[band],
            recv_sem=back_recv.at[band],
            device_id={"lat": lat, "lon": west},
            device_id_type=MESH,
        )

    lane = lax.broadcasted_iota(jnp.int32, (1, 128), 1)
    low = lane < HEAD_DIM
    mine = []
    for band in range(2):
        present, copies = ((has_north, to_south), (has_south, to_north))[band]

        @pl.when(present)
        def _():
            for copy in copies:
                copy.wait_recv()

        normed = norm(flat(halo[6 * band : 6 * band + 6]).astype(F32), gain_attn[...])
        normed_q = normed[144:288] if band == 0 else normed[0:144]
        q = (dot(normed_q, w_qkv[:, 0:D]) * HEAD_DIM**-0.5).astype(BF16)
        k = dot(normed, w_qkv[:, D : 2 * D]).astype(BF16)
        v = dot(normed, w_qkv[:, 2 * D : 3 * D]).astype(BF16)
        parts = []
        for pair in range(HEADS // 2):
            cols = slice(128 * pair, 128 * pair + 128)
            q_pair, k_pair, v_pair = q[:, cols], k[:, cols], v[:, cols]
            outs = []
            for first in (True, False):
                keep = low if first else jnp.logical_not(low)
                scores = dot_t(q_pair, jnp.where(keep, k_pair, jnp.zeros_like(k_pair))) + bias[band]
                raised = jnp.exp(scores - jnp.max(scores, axis=-1, keepdims=True))
                total = jnp.sum(raised, axis=-1, keepdims=True)
                weights = (raised * (1.0 / total)).astype(BF16)
                outs.append(dot(weights, v_pair))
            parts.append(jnp.where(low, outs[0], outs[1]))
        attended = jnp.concatenate(parts, axis=1).astype(BF16).reshape(3, 12, 4, D)
        back[band] = attended[:, 0:6]
        give_back(band).start()
        mine.append(flat(attended[:, 6:12]))

    loads[3].wait()
    loads[4].wait()
    loads[5].wait()
    for half in range(2):
        if half == 0:
            attended = jnp.concatenate(mine, axis=0)
        else:
            give_back(0).wait_recv()
            give_back(1).wait_recv()
            attended = jnp.concatenate([flat(got[0]), flat(got[1])], axis=0)
        cols = slice(6 * half, 6 * half + 6)
        residual = (flat(xv[:, cols]).astype(F32) + dot(attended, w_out[...])).astype(BF16).astype(F32)
        hidden = gelu(dot(norm(residual, gain_mlp[...]), w_up[...])).astype(BF16)
        block = (residual + dot(hidden, w_down[...])).astype(BF16)
        o_ref[:, cols] = block.reshape(6, 6, 4, D)

    to_east.wait_send()

    @pl.when(has_north)
    def _():
        for copy in to_north:
            copy.wait_send()

    @pl.when(has_south)
    def _():
        for copy in to_south:
            copy.wait_send()

    give_back(0).wait_send()
    give_back(1).wait_send()


def solution(mesh):
    n_lat, n_lon = mesh.shape["lat"], mesh.shape["lon"]

    def body(tokens, gain_attn, w_qkv, w_out, gain_mlp, w_up, w_down):
        x = tokens.transpose(1, 2, 0, 3)
        hbm = pl.BlockSpec(memory_space=pltpu.HBM)
        vmem = pl.BlockSpec(memory_space=pltpu.VMEM)
        out = pl.pallas_call(
            functools.partial(kernel, n_lat, n_lon),
            out_shape=jax.ShapeDtypeStruct(x.shape, BF16),
            in_specs=[hbm, vmem, hbm, hbm, vmem, hbm, hbm],
            out_specs=vmem,
            scratch_shapes=[
                pltpu.VMEM((6, 12, 4, D), BF16),
                pltpu.VMEM((12, 12, 4, D), BF16),
                pltpu.VMEM((2, 3, 6, 4, D), BF16),
                pltpu.VMEM((2, 3, 6, 4, D), BF16),
                pltpu.VMEM((2, 144, 288), F32),
                pltpu.VMEM((D, 3 * D), BF16),
                pltpu.VMEM((D, D), BF16),
                pltpu.VMEM((D, FF), BF16),
                pltpu.VMEM((FF, D), BF16),
                pltpu.SemaphoreType.DMA((5,)),
                pltpu.SemaphoreType.DMA((5,)),
                pltpu.SemaphoreType.DMA((2,)),
                pltpu.SemaphoreType.DMA((2,)),
                pltpu.SemaphoreType.DMA((4,)),
                pltpu.SemaphoreType.DMA((2,)),
            ],
            compiler_params=pltpu.CompilerParams(
                collective_id=0, has_side_effects=True, vmem_limit_bytes=58 * 1024 * 1024
            ),
            cost_estimate=pl.CostEstimate(flops=2_500_000_000, bytes_accessed=7_000_000, transcendentals=1_500_000),
        )(x, gain_attn.reshape(1, D), w_qkv, w_out, gain_mlp.reshape(1, D), w_up, w_down)
        return out.transpose(2, 0, 1, 3)

    in_specs = (P(None, "lat", "lon", None), P(), P(), P(), P(), P(), P())
    out_specs = P(None, "lat", "lon", None)
    return jax.shard_map(body, mesh=mesh, in_specs=in_specs, out_specs=out_specs, check_vma=False)
```

```python
import functools

import jax
import jax.numpy as jnp
from jax import lax
from jax.experimental import pallas as pl
from jax.experimental.pallas import tpu as pltpu
from jax.sharding import PartitionSpec as P

HEADS = 8
D = 512
FF = 2048
HEAD_DIM = 64
F32 = jnp.float32
BF16 = jnp.bfloat16
MESH = pl.DeviceIdType.MESH


def norm32(values, gain):
    average = jnp.mean(values, axis=-1, keepdims=True)
    centered = values - average
    spread = jnp.mean(centered * centered, axis=-1, keepdims=True)
    return centered * lax.rsqrt(spread + 1e-05) * gain


def norm(values, gain):
    return norm32(values, gain).astype(BF16)


def inner_levels(shape):
    place = lax.rem(lax.broadcasted_iota(jnp.int32, shape, 1), 4)
    return (place == 1) | (place == 2)


def split_levels(values):
    pairs = values.reshape(values.shape[0] // 16, 2, 8, values.shape[1])
    first, second = pairs[:, 0], pltpu.roll(pairs[:, 1], 2, 1)
    inner = inner_levels(first.shape)
    half = (values.shape[0] // 2, values.shape[1])
    return jnp.where(inner, first, second).reshape(half), jnp.where(inner, second, first).reshape(half)


def join_levels(inner_half, outer_half):
    shape = (inner_half.shape[0] // 8, 8, inner_half.shape[1])
    a, b = inner_half.reshape(shape), outer_half.reshape(shape)
    inner = inner_levels(shape)
    first, second = jnp.where(inner, a, b), pltpu.roll(jnp.where(inner, b, a), 6, 1)
    return jnp.stack([first, second], axis=1).reshape(2 * inner_half.shape[0], inner_half.shape[1])


def flat(block):
    rows = block.shape[0] * block.shape[1] * block.shape[2]
    return block.reshape(rows, block.shape[3])


def gelu(v):
    inner = v * (0.7978845608028654 + 0.035677408136300125 * (v * v))
    return (0.5 * v) * (1.0 + jnp.tanh(inner))


def dot(a, b):
    return jnp.dot(a, b, preferred_element_type=F32)


def dot_t(a, b):
    return lax.dot_general(a, b, (((1,), (1,)), ((), ())), preferred_element_type=F32)


def kernel(
    n_lat,
    n_lon,
    x_hbm,
    gain_attn,
    w_qkv_hbm,
    w_out_hbm,
    gain_mlp,
    w_up_hbm,
    w_down_hbm,
    o_ref,
    xv,
    halo,
    back,
    got,
    mine,
    bias,
    w_qkv,
    w_out,
    w_up,
    w_down,
    send_sem,
    recv_sem,
    back_send,
    back_recv,
    w_sem,
    x_sem,
):
    lat = lax.axis_index("lat")
    lon = lax.axis_index("lon")
    west = lax.rem(lon + n_lon - 1, n_lon)
    east = lax.rem(lon + 1, n_lon)
    has_north = lat > 0
    has_south = lat < n_lat - 1

    barrier = pltpu.get_barrier_semaphore()

    def greet(la, lo):
        pl.semaphore_signal(barrier, inc=1, device_id={"lat": la, "lon": lo}, device_id_type=MESH)

    greet(lat, west)

    @pl.when(has_north)
    def _():
        greet(lat - 1, lon)
        greet(lat - 1, west)

    @pl.when(has_south)
    def _():
        greet(lat + 1, lon)
        greet(lat + 1, west)

    loads = [
        pltpu.make_async_copy(x_hbm, xv, x_sem.at[0]),
        pltpu.make_async_copy(x_hbm.at[:, 0:6], halo.at[3:9, 6:12], x_sem.at[1]),
        pltpu.make_async_copy(w_qkv_hbm, w_qkv, w_sem.at[0]),
        pltpu.make_async_copy(w_out_hbm, w_out, w_sem.at[1]),
        pltpu.make_async_copy(w_up_hbm, w_up, w_sem.at[2]),
        pltpu.make_async_copy(w_down_hbm, w_down, w_sem.at[3]),
    ]
    for load in loads:
        load.start()

    def send(index, src, dst, la, lo):
        return pltpu.make_async_remote_copy(
            src_ref=src,
            dst_ref=dst,
            send_sem=send_sem.at[index],
            recv_sem=recv_sem.at[index],
            device_id={"lat": la, "lon": lo},
            device_id_type=MESH,
        )

    to_east = send(0, x_hbm.at[:, 6:12], halo.at[3:9, 0:6], lat, east)
    to_north = [
        send(1, x_hbm.at[0:3, 0:6], halo.at[9:12, 6:12], lat - 1, lon),
        send(2, x_hbm.at[0:3, 6:12], halo.at[9:12, 0:6], lat - 1, east),
    ]
    to_south = [
        send(3, x_hbm.at[3:6, 0:6], halo.at[0:3, 6:12], lat + 1, lon),
        send(4, x_hbm.at[3:6, 6:12], halo.at[0:3, 0:6], lat + 1, east),
    ]

    pl.semaphore_wait(barrier, 1 + 2 * (has_north.astype(jnp.int32) + has_south.astype(jnp.int32)))
    to_east.start()

    @pl.when(has_north)
    def _():
        for copy in to_north:
            copy.start()

    @pl.when(has_south)
    def _():
        for copy in to_south:
            copy.start()

    key = lax.broadcasted_iota(jnp.int32, (288, 144), 1)
    query = lax.broadcasted_iota(jnp.int32, (288, 144), 0)
    same = lax.rem(key + query, 2) == 0
    for band, known in enumerate(((key >= 72) | has_north, (key < 72) | has_south)):
        bias[band, 0] = jnp.where(known, 0.0, -1e30)
        bias[band, 1] = jnp.where(known & same, 0.0, -1e30)

    @pl.when(jnp.logical_not(has_north))
    def _():
        halo[0:3] = jnp.zeros((3, 12, 4, D), BF16)

    @pl.when(jnp.logical_not(has_south))
    def _():
        halo[9:12] = jnp.zeros((3, 12, 4, D), BF16)

    loads[0].wait()
    loads[1].wait()
    loads[2].wait()
    to_east.wait_recv()

    def give_back(band):
        return pltpu.make_async_remote_copy(
            src_ref=back.at[band],
            dst_ref=got.at[band],
            send_sem=back_send.at[band],
            recv_sem=back_recv.at[band],
            device_id={"lat": lat, "lon": west},
            device_id_type=MESH,
        )

    head = lax.div(lax.broadcasted_iota(jnp.int32, (72, 256), 1), HEAD_DIM)
    first = (lat >= n_lat // 2).astype(jnp.int32)
    for step in range(2):
        band = first if step == 0 else 1 - first

        @pl.when((band == 0) & has_north)
        def _():
            for copy in to_south:
                copy.wait_recv()

        @pl.when((band == 1) & has_south)
        def _():
            for copy in to_north:
                copy.wait_recv()

        normed = split_levels(norm32(flat(halo[pl.ds(6 * band, 6)]).astype(F32), gain_attn[...]))
        mixed = []
        for group in range(2):
            tokens = normed[group].astype(BF16)
            own = jnp.where(band == 0, normed[group][72:144], normed[group][0:72]).astype(BF16)
            q = (dot(own, w_qkv[:, 0:D]) * HEAD_DIM**-0.5).astype(BF16)
            k = dot(tokens, w_qkv[:, D : 2 * D]).astype(BF16)
            v = dot(tokens, w_qkv[:, 2 * D : 3 * D]).astype(BF16)
            parts = []
            for quad in range(2):
                cols = slice(256 * quad, 256 * quad + 256)
                q_quad = q[:, cols]
                zero = jnp.zeros_like(q_quad)
                stacked = jnp.concatenate([jnp.where(head == h, q_quad, zero) for h in range(4)], axis=0)
                scores = dot_t(stacked, k[:, cols]) + bias[band, group]
                raised = jnp.exp(scores - jnp.max(scores, axis=-1, keepdims=True))
                total = jnp.sum(raised, axis=-1, keepdims=True)
                weights = (raised * (1.0 / total)).astype(BF16)
                out = dot(weights, v[:, cols])
                part = out[0:72]
                for h in range(1, 4):
                    part = jnp.where(head == h, out[72 * h : 72 * h + 72], part)
                parts.append(part)
            mixed.append(jnp.concatenate(parts, axis=1))
        attended = join_levels(*mixed).astype(BF16).reshape(3, 12, 4, D)
        back[band] = attended[:, 0:6]
        give_back(band).start()
        mine[band] = attended[:, 6:12]

    loads[3].wait()
    loads[4].wait()
    loads[5].wait()
    for half in range(2):
        if half == 0:
            attended = jnp.concatenate([flat(mine[0]), flat(mine[1])], axis=0)
        else:
            give_back(0).wait_recv()
            give_back(1).wait_recv()
            attended = jnp.concatenate([flat(got[0]), flat(got[1])], axis=0)
        cols = slice(6 * half, 6 * half + 6)
        residual = (flat(xv[:, cols]).astype(F32) + dot(attended, w_out[...])).astype(BF16).astype(F32)
        hidden = gelu(dot(norm(residual, gain_mlp[...]), w_up[...])).astype(BF16)
        block = (residual + dot(hidden, w_down[...])).astype(BF16)
        o_ref[:, cols] = block.reshape(6, 6, 4, D)

    to_east.wait_send()

    @pl.when(has_north)
    def _():
        for copy in to_north:
            copy.wait_send()

    @pl.when(has_south)
    def _():
        for copy in to_south:
            copy.wait_send()

    give_back(0).wait_send()
    give_back(1).wait_send()


def solution(mesh):
    n_lat, n_lon = mesh.shape["lat"], mesh.shape["lon"]

    def body(tokens, gain_attn, w_qkv, w_out, gain_mlp, w_up, w_down):
        x = tokens.transpose(1, 2, 0, 3)
        hbm = pl.BlockSpec(memory_space=pltpu.HBM)
        vmem = pl.BlockSpec(memory_space=pltpu.VMEM)
        out = pl.pallas_call(
            functools.partial(kernel, n_lat, n_lon),
            out_shape=jax.ShapeDtypeStruct(x.shape, BF16),
            in_specs=[hbm, vmem, hbm, hbm, vmem, hbm, hbm],
            out_specs=vmem,
            scratch_shapes=[
                pltpu.VMEM((6, 12, 4, D), BF16),
                pltpu.VMEM((12, 12, 4, D), BF16),
                pltpu.VMEM((2, 3, 6, 4, D), BF16),
                pltpu.VMEM((2, 3, 6, 4, D), BF16),
                pltpu.VMEM((2, 3, 6, 4, D), BF16),
                pltpu.VMEM((2, 2, 288, 144), F32),
                pltpu.VMEM((D, 3 * D), BF16),
                pltpu.VMEM((D, D), BF16),
                pltpu.VMEM((D, FF), BF16),
                pltpu.VMEM((FF, D), BF16),
                pltpu.SemaphoreType.DMA((5,)),
                pltpu.SemaphoreType.DMA((5,)),
                pltpu.SemaphoreType.DMA((2,)),
                pltpu.SemaphoreType.DMA((2,)),
                pltpu.SemaphoreType.DMA((4,)),
                pltpu.SemaphoreType.DMA((2,)),
            ],
            compiler_params=pltpu.CompilerParams(
                collective_id=0, has_side_effects=True, vmem_limit_bytes=58 * 1024 * 1024
            ),
            cost_estimate=pl.CostEstimate(flops=2_500_000_000, bytes_accessed=7_000_000, transcendentals=1_500_000),
        )(x, gain_attn.reshape(1, D), w_qkv, w_out, gain_mlp.reshape(1, D), w_up, w_down)
        return out.transpose(2, 0, 1, 3)

    in_specs = (P(None, "lat", "lon", None), P(), P(), P(), P(), P(), P())
    out_specs = P(None, "lat", "lon", None)
    return jax.shard_map(body, mesh=mesh, in_specs=in_specs, out_specs=out_specs, check_vma=False)
```

```python
import functools

import jax
import jax.numpy as jnp
from jax import lax
from jax.experimental import pallas as pl
from jax.experimental.pallas import tpu as pltpu
from jax.sharding import PartitionSpec as P

HEADS = 8
D = 512
FF = 2048
HEAD_DIM = 64
F32 = jnp.float32
BF16 = jnp.bfloat16
MESH = pl.DeviceIdType.MESH


def norm32(values, gain):
    average = jnp.mean(values, axis=-1, keepdims=True)
    centered = values - average
    spread = jnp.mean(centered * centered, axis=-1, keepdims=True)
    return centered * lax.rsqrt(spread + 1e-05) * gain


def norm(values, gain):
    return norm32(values, gain).astype(BF16)


def inner_levels(shape):
    place = lax.rem(lax.broadcasted_iota(jnp.int32, shape, 1), 4)
    return (place == 1) | (place == 2)


def split_levels(values):
    pairs = values.reshape(values.shape[0] // 16, 2, 8, values.shape[1])
    first, second = pairs[:, 0], pltpu.roll(pairs[:, 1], 2, 1)
    inner = inner_levels(first.shape)
    half = (values.shape[0] // 2, values.shape[1])
    return jnp.where(inner, first, second).reshape(half), jnp.where(inner, second, first).reshape(half)


def join_levels(inner_half, outer_half):
    shape = (inner_half.shape[0] // 8, 8, inner_half.shape[1])
    a, b = inner_half.reshape(shape), outer_half.reshape(shape)
    inner = inner_levels(shape)
    first, second = jnp.where(inner, a, b), pltpu.roll(jnp.where(inner, b, a), 6, 1)
    return jnp.stack([first, second], axis=1).reshape(2 * inner_half.shape[0], inner_half.shape[1])


def flat(block):
    rows = block.shape[0] * block.shape[1] * block.shape[2]
    return block.reshape(rows, block.shape[3])


def gelu(v):
    inner = v * (0.7978845608028654 + 0.035677408136300125 * (v * v))
    return (0.5 * v) * (1.0 + jnp.tanh(inner))


def dot(a, b):
    return jnp.dot(a, b, preferred_element_type=F32)


def dot_t(a, b):
    return lax.dot_general(a, b, (((1,), (1,)), ((), ())), preferred_element_type=F32)


def feed_forward(attended, x, w_out, gain, w_up, w_down):
    residual = (flat(x).astype(F32) + dot(attended, w_out[...])).astype(BF16).astype(F32)
    hidden = gelu(dot(norm(residual, gain[...]), w_up[...])).astype(BF16)
    block = (residual + dot(hidden, w_down[...])).astype(BF16)
    return block.reshape(x.shape)


def finish(early, late, xv, w_out, gain, w_up, w_down, o_hbm, done, sem):
    put = pltpu.make_async_copy(early, o_hbm.at[:, 0:6], sem.at[0])
    put.start()
    done[...] = feed_forward(flat(late[...]), xv[:, 6:12], w_out, gain, w_up, w_down)
    last = pltpu.make_async_copy(done, o_hbm.at[:, 6:12], sem.at[1])
    last.start()
    put.wait()
    last.wait()


def kernel(
    n_lat,
    n_lon,
    x_hbm,
    gain_attn_hbm,
    w_qkv_hbm,
    w_out_hbm,
    gain_mlp_hbm,
    w_up_hbm,
    w_down_hbm,
    early,
    late,
    xv,
    w_out,
    gain_mlp,
    w_up,
    w_down,
    gain_attn,
    halo,
    back,
    got,
    mine,
    bias,
    w_qkv,
    send_sem,
    recv_sem,
    back_send,
    back_recv,
    w_sem,
    x_sem,
    ok_sem,
):
    lat = lax.axis_index("lat")
    lon = lax.axis_index("lon")
    west = lax.rem(lon + n_lon - 1, n_lon)
    east = lax.rem(lon + 1, n_lon)
    has_north = lat > 0
    has_south = lat < n_lat - 1

    barrier = pltpu.get_barrier_semaphore()

    def greet(la, lo):
        pl.semaphore_signal(barrier, inc=1, device_id={"lat": la, "lon": lo}, device_id_type=MESH)

    middle = n_lat // 2

    def at_once(sender_lon, far):
        return far | (lax.rem(sender_lon, 2) == 0) | (lax.rem(sender_lon, n_lon // 2) == n_lon // 2 - 1)

    far_north, far_south = lat == middle, lat == middle - 1
    greet(lat, west)
    for present, far, other in ((has_north, far_north, lat - 1), (has_south, far_south, lat + 1)):

        @pl.when(present)
        def _():
            greet(other, lon)

        @pl.when(present & at_once(west, far))
        def _():
            greet(other, west)

    loads = [
        pltpu.make_async_copy(x_hbm, xv, x_sem.at[0]),
        pltpu.make_async_copy(x_hbm.at[:, 0:6], halo.at[3:9, 6:12], x_sem.at[1]),
        pltpu.make_async_copy(gain_attn_hbm, gain_attn, w_sem.at[4]),
        pltpu.make_async_copy(w_qkv_hbm, w_qkv, w_sem.at[0]),
        pltpu.make_async_copy(gain_mlp_hbm, gain_mlp, w_sem.at[5]),
        pltpu.make_async_copy(w_out_hbm, w_out, w_sem.at[1]),
        pltpu.make_async_copy(w_up_hbm, w_up, w_sem.at[2]),
        pltpu.make_async_copy(w_down_hbm, w_down, w_sem.at[3]),
    ]
    for load in loads:
        load.start()

    def send(index, src, dst, la, lo):
        return pltpu.make_async_remote_copy(
            src_ref=src,
            dst_ref=dst,
            send_sem=send_sem.at[index],
            recv_sem=recv_sem.at[index],
            device_id={"lat": la, "lon": lo},
            device_id_type=MESH,
        )

    to_east = send(0, x_hbm.at[:, 6:12], halo.at[3:9, 0:6], lat, east)
    to_north = [
        send(1, x_hbm.at[0:3, 0:6], halo.at[9:12, 6:12], lat - 1, lon),
        send(2, x_hbm.at[0:3, 6:12], halo.at[9:12, 0:6], lat - 1, east),
    ]
    to_south = [
        send(3, x_hbm.at[3:6, 0:6], halo.at[0:3, 6:12], lat + 1, lon),
        send(4, x_hbm.at[3:6, 6:12], halo.at[0:3, 0:6], lat + 1, east),
    ]

    ways = ((has_north, far_north, lat - 1, 0, to_north), (has_south, far_south, lat + 1, 1, to_south))
    greetings = 1
    for present, far, _, _, _ in ways:
        greetings += present.astype(jnp.int32) + (present & at_once(lon, far)).astype(jnp.int32)
    pl.semaphore_wait(barrier, greetings)
    to_east.start()
    for present, far, other, way, copies in ways:

        @pl.when(present)
        def _():
            copies[0].start()

        @pl.when(present & jnp.logical_not(at_once(lon, far)))
        def _():
            pl.semaphore_signal(
                ok_sem.at[1 - way], inc=1, device_id={"lat": other, "lon": lon}, device_id_type=MESH
            )

        @pl.when(present & at_once(lon, far))
        def _():
            copies[1].start()

    for present, far, other, way, copies in ways:

        @pl.when(present & jnp.logical_not(at_once(lon, far)))
        def _():
            pl.semaphore_wait(ok_sem.at[way], 1)
            copies[1].start()

    key = lax.broadcasted_iota(jnp.int32, (288, 144), 1)
    query = lax.broadcasted_iota(jnp.int32, (288, 144), 0)
    same = lax.rem(key + query, 2) == 0
    for band, known in enumerate(((key >= 72) | has_north, (key < 72) | has_south)):
        bias[band, 0] = jnp.where(known, 0.0, -1e30)
        bias[band, 1] = jnp.where(known & same, 0.0, -1e30)

    @pl.when(jnp.logical_not(has_north))
    def _():
        halo[0:3] = jnp.zeros((3, 12, 4, D), BF16)

    @pl.when(jnp.logical_not(has_south))
    def _():
        halo[9:12] = jnp.zeros((3, 12, 4, D), BF16)

    def give_back(band):
        return pltpu.make_async_remote_copy(
            src_ref=back.at[band],
            dst_ref=got.at[band],
            send_sem=back_send.at[band],
            recv_sem=back_recv.at[band],
            device_id={"lat": lat, "lon": west},
            device_id_type=MESH,
        )

    loads[0].wait()
    loads[1].wait()
    loads[2].wait()
    loads[3].wait()

    to_east.wait_recv()

    head = lax.div(lax.broadcasted_iota(jnp.int32, (72, 256), 1), HEAD_DIM)
    first = (lat >= n_lat // 2).astype(jnp.int32)
    for step in range(2):
        band = first if step == 0 else 1 - first

        @pl.when((band == 0) & has_north)
        def _():
            for copy in to_south:
                copy.wait_recv()

        @pl.when((band == 1) & has_south)
        def _():
            for copy in to_north:
                copy.wait_recv()

        normed = split_levels(norm32(flat(halo[pl.ds(6 * band, 6)]).astype(F32), gain_attn[...]))
        mixed = []
        for group in range(2):
            tokens = normed[group].astype(BF16)
            own = jnp.where(band == 0, normed[group][72:144], normed[group][0:72]).astype(BF16)
            q = (dot(own, w_qkv[:, 0:D]) * HEAD_DIM**-0.5).astype(BF16)
            k = dot(tokens, w_qkv[:, D : 2 * D]).astype(BF16)
            v = dot(tokens, w_qkv[:, 2 * D : 3 * D]).astype(BF16)
            parts = []
            for quad in range(2):
                cols = slice(256 * quad, 256 * quad + 256)
                q_quad = q[:, cols]
                zero = jnp.zeros_like(q_quad)
                stacked = jnp.concatenate([jnp.where(head == h, q_quad, zero) for h in range(4)], axis=0)
                scores = dot_t(stacked, k[:, cols]) + bias[band, group]
                raised = jnp.exp(scores - jnp.max(scores, axis=-1, keepdims=True))
                total = jnp.sum(raised, axis=-1, keepdims=True)
                weights = (raised * (1.0 / total)).astype(BF16)
                out = dot(weights, v[:, cols])
                part = out[0:72]
                for h in range(1, 4):
                    part = jnp.where(head == h, out[72 * h : 72 * h + 72], part)
                parts.append(part)
            mixed.append(jnp.concatenate(parts, axis=1))
        attended = join_levels(*mixed).astype(BF16).reshape(3, 12, 4, D)
        back[band] = attended[:, 0:6]
        give_back(band).start()
        mine[band] = attended[:, 6:12]

    for load in loads[4:]:
        load.wait()
    early[...] = feed_forward(
        jnp.concatenate([flat(mine[0]), flat(mine[1])], axis=0), xv[:, 0:6], w_out, gain_mlp, w_up, w_down
    )
    for band in range(2):
        give_back(band).wait_recv()
        late[3 * band : 3 * band + 3] = got[band]

    to_east.wait_send()

    @pl.when(has_north)
    def _():
        for copy in to_north:
            copy.wait_send()

    @pl.when(has_south)
    def _():
        for copy in to_south:
            copy.wait_send()

    give_back(0).wait_send()
    give_back(1).wait_send()


def solution(mesh):
    n_lat, n_lon = mesh.shape["lat"], mesh.shape["lon"]

    def body(tokens, gain_attn, w_qkv, w_out, gain_mlp, w_up, w_down):
        x = tokens.transpose(1, 2, 0, 3)
        gain_attn, gain_mlp = gain_attn.reshape(1, D), gain_mlp.reshape(1, D)
        hbm = pl.BlockSpec(memory_space=pltpu.HBM)
        vmem = pl.BlockSpec(memory_space=pltpu.VMEM)
        held = [
            pltpu.with_memory_space_constraint(a, pltpu.HBM)
            for a in (x, gain_attn, w_qkv, w_out, gain_mlp, w_up, w_down)
        ]
        half = jax.ShapeDtypeStruct((6, 6, 4, D), BF16)
        passed = [jax.ShapeDtypeStruct(a.shape, a.dtype) for a in (x, w_out, gain_mlp, w_up, w_down)]
        made = pl.pallas_call(
            functools.partial(kernel, n_lat, n_lon),
            out_shape=[half, half] + passed,
            in_specs=[hbm] * 7,
            out_specs=[vmem] * 7,
            scratch_shapes=[
                pltpu.VMEM((1, D), F32),
                pltpu.VMEM((12, 12, 4, D), BF16),
                pltpu.VMEM((2, 3, 6, 4, D), BF16),
                pltpu.VMEM((2, 3, 6, 4, D), BF16),
                pltpu.VMEM((2, 3, 6, 4, D), BF16),
                pltpu.VMEM((2, 2, 288, 144), F32),
                pltpu.VMEM((D, 3 * D), BF16),
                pltpu.SemaphoreType.DMA((5,)),
                pltpu.SemaphoreType.DMA((5,)),
                pltpu.SemaphoreType.DMA((2,)),
                pltpu.SemaphoreType.DMA((2,)),
                pltpu.SemaphoreType.DMA((6,)),
                pltpu.SemaphoreType.DMA((2,)),
                pltpu.SemaphoreType.REGULAR((2,)),
            ],
            compiler_params=pltpu.CompilerParams(
                collective_id=0, has_side_effects=True, vmem_limit_bytes=40 * 1024 * 1024
            ),
            cost_estimate=pl.CostEstimate(flops=1_800_000_000, bytes_accessed=7_000_000, transcendentals=1_000_000),
        )(*held)
        out = pl.pallas_call(
            finish,
            out_shape=jax.ShapeDtypeStruct(x.shape, BF16),
            in_specs=[vmem] * 7,
            out_specs=hbm,
            scratch_shapes=[pltpu.VMEM((6, 6, 4, D), BF16), pltpu.SemaphoreType.DMA((2,))],
            compiler_params=pltpu.CompilerParams(vmem_limit_bytes=40 * 1024 * 1024),
            cost_estimate=pl.CostEstimate(flops=700_000_000, bytes_accessed=300_000, transcendentals=300_000),
        )(*made)
        return out.transpose(2, 0, 1, 3)

    in_specs = (P(None, "lat", "lon", None), P(), P(), P(), P(), P(), P())
    out_specs = P(None, "lat", "lon", None)
    return jax.shard_map(body, mesh=mesh, in_specs=in_specs, out_specs=out_specs, check_vma=False)
```

```python
import functools

import jax
import jax.numpy as jnp
from jax import lax
from jax.experimental import pallas as pl
from jax.experimental.pallas import tpu as pltpu
from jax.sharding import PartitionSpec as P

HEADS = 8
D = 512
FF = 2048
HEAD_DIM = 64
F32 = jnp.float32
BF16 = jnp.bfloat16
MESH = pl.DeviceIdType.MESH


def norm32(values, gain):
    average = jnp.mean(values, axis=-1, keepdims=True)
    centered = values - average
    spread = jnp.mean(centered * centered, axis=-1, keepdims=True)
    return centered * lax.rsqrt(spread + 1e-05) * gain


def norm(values, gain):
    return norm32(values, gain).astype(BF16)


def inner_levels(shape):
    place = lax.rem(lax.broadcasted_iota(jnp.int32, shape, 1), 4)
    return (place == 1) | (place == 2)


def split_levels(values):
    pairs = values.reshape(values.shape[0] // 16, 2, 8, values.shape[1])
    first, second = pairs[:, 0], pltpu.roll(pairs[:, 1], 2, 1)
    inner = inner_levels(first.shape)
    half = (values.shape[0] // 2, values.shape[1])
    return jnp.where(inner, first, second).reshape(half), jnp.where(inner, second, first).reshape(half)


def join_levels(inner_half, outer_half):
    shape = (inner_half.shape[0] // 8, 8, inner_half.shape[1])
    a, b = inner_half.reshape(shape), outer_half.reshape(shape)
    inner = inner_levels(shape)
    first, second = jnp.where(inner, a, b), pltpu.roll(jnp.where(inner, b, a), 6, 1)
    return jnp.stack([first, second], axis=1).reshape(2 * inner_half.shape[0], inner_half.shape[1])


def flat(block):
    rows = block.shape[0] * block.shape[1] * block.shape[2]
    return block.reshape(rows, block.shape[3])


def gelu(v):
    inner = v * (0.7978845608028654 + 0.035677408136300125 * (v * v))
    return (0.5 * v) * (1.0 + jnp.tanh(inner))


def dot(a, b):
    return jnp.dot(a, b, preferred_element_type=F32)


def dot_t(a, b):
    return lax.dot_general(a, b, (((1,), (1,)), ((), ())), preferred_element_type=F32)


def feed_forward(attended, x, w_out, gain, w_up, w_down):
    residual = (flat(x).astype(F32) + dot(attended, w_out[...])).astype(BF16).astype(F32)
    hidden = gelu(dot(norm(residual, gain[...]), w_up[...])).astype(BF16)
    block = (residual + dot(hidden, w_down[...])).astype(BF16)
    return block.reshape(x.shape)


def finish(early, late, xv, w_out, gain, w_up, w_down, o_hbm, done, sem):
    put = pltpu.make_async_copy(early, o_hbm.at[:, 0:6], sem.at[0])
    put.start()
    done[...] = feed_forward(flat(late[...]), xv[:, 6:12], w_out, gain, w_up, w_down)
    last = pltpu.make_async_copy(done, o_hbm.at[:, 6:12], sem.at[1])
    last.start()
    put.wait()
    last.wait()


def kernel(
    n_lat,
    n_lon,
    x_hbm,
    gain_attn_hbm,
    w_qkv_hbm,
    w_out_hbm,
    gain_mlp_hbm,
    w_up_hbm,
    w_down_hbm,
    early,
    late,
    xv,
    w_out,
    gain_mlp,
    w_up,
    w_down,
    gain_attn,
    halo,
    made,
    own,
    got,
    bias,
    w_qkv,
    send_sem,
    recv_sem,
    back_send,
    back_recv,
    w_sem,
    x_sem,
    ok_sem,
):
    lat = lax.axis_index("lat")
    lon = lax.axis_index("lon")
    west = lax.rem(lon + n_lon - 1, n_lon)
    east = lax.rem(lon + 1, n_lon)
    has_north = lat > 0
    has_south = lat < n_lat - 1

    barrier = pltpu.get_barrier_semaphore()

    def greet(la, lo):
        pl.semaphore_signal(barrier, inc=1, device_id={"lat": la, "lon": lo}, device_id_type=MESH)

    middle = n_lat // 2

    def at_once(sender_lon, far):
        return far | (lax.rem(sender_lon, 2) == 0) | (lax.rem(sender_lon, n_lon // 2) == n_lon // 2 - 1)

    far_north, far_south = lat == middle, lat == middle - 1
    even = lax.rem(lon, 2) == 0
    seven, eight = lax.rem(lon, n_lon // 2) == n_lon // 4 - 1, lax.rem(lon, n_lon // 2) == n_lon // 4
    greet(lat, west)

    @pl.when(seven)
    def _():
        greet(lat, east)

    for present, far, other in ((has_north, far_north, lat - 1), (has_south, far_south, lat + 1)):

        @pl.when(present & even)
        def _():
            greet(other, lon)

        @pl.when(present & at_once(west, far))
        def _():
            greet(other, west)

        @pl.when(present & seven)
        def _():
            greet(other, east)

    loads = [
        pltpu.make_async_copy(x_hbm, xv, x_sem.at[0]),
        pltpu.make_async_copy(x_hbm.at[:, 0:6], halo.at[0, 3:9, 6:12], x_sem.at[1]),
        pltpu.make_async_copy(x_hbm.at[:, 6:12], halo.at[1, 3:9, 0:6], x_sem.at[2]),
        pltpu.make_async_copy(gain_attn_hbm, gain_attn, w_sem.at[4]),
        pltpu.make_async_copy(w_qkv_hbm, w_qkv, w_sem.at[0]),
        pltpu.make_async_copy(gain_mlp_hbm, gain_mlp, w_sem.at[5]),
        pltpu.make_async_copy(w_out_hbm, w_out, w_sem.at[1]),
        pltpu.make_async_copy(w_up_hbm, w_up, w_sem.at[2]),
        pltpu.make_async_copy(w_down_hbm, w_down, w_sem.at[3]),
    ]
    for load in loads:
        load.start()

    def send(index, src, dst, la, lo):
        return pltpu.make_async_remote_copy(
            src_ref=src,
            dst_ref=dst,
            send_sem=send_sem.at[index],
            recv_sem=recv_sem.at[index],
            device_id={"lat": la, "lon": lo},
            device_id_type=MESH,
        )

    to_east = send(0, x_hbm.at[:, 6:12], halo.at[0, 3:9, 0:6], lat, east)
    to_north = [
        send(1, x_hbm.at[0:3, 0:6], halo.at[0, 9:12, 6:12], lat - 1, lon),
        send(2, x_hbm.at[0:3, 6:12], halo.at[0, 9:12, 0:6], lat - 1, east),
    ]
    to_south = [
        send(3, x_hbm.at[3:6, 0:6], halo.at[0, 0:3, 6:12], lat + 1, lon),
        send(4, x_hbm.at[3:6, 6:12], halo.at[0, 0:3, 0:6], lat + 1, east),
    ]
    to_west = send(5, x_hbm.at[:, 0:6], halo.at[1, 3:9, 6:12], lat, west)
    to_north_2 = [
        send(6, x_hbm.at[0:3, 6:12], halo.at[1, 9:12, 0:6], lat - 1, lon),
        send(7, x_hbm.at[0:3, 0:6], halo.at[1, 9:12, 6:12], lat - 1, west),
    ]
    to_south_2 = [
        send(8, x_hbm.at[3:6, 6:12], halo.at[1, 0:3, 0:6], lat + 1, lon),
        send(9, x_hbm.at[3:6, 0:6], halo.at[1, 0:3, 6:12], lat + 1, west),
    ]

    ways = (
        (has_north, far_north, lat - 1, 0, to_north, to_north_2),
        (has_south, far_south, lat + 1, 1, to_south, to_south_2),
    )
    greetings = 1 + eight.astype(jnp.int32)
    for present, far, *_ in ways:
        for greets in (even, at_once(lon, far), eight):
            greetings += (present & greets).astype(jnp.int32)
    pl.semaphore_wait(barrier, greetings)

    @pl.when(even)
    def _():
        pl.semaphore_signal(ok_sem.at[2], inc=1, device_id={"lat": lat, "lon": east}, device_id_type=MESH)

    to_east.start()

    @pl.when(eight)
    def _():
        to_west.start()

    for present, far, other, way, copies, copies_2 in ways:

        @pl.when(present & at_once(lon, far))
        def _():
            copies[1].start()

        @pl.when(present & eight)
        def _():
            copies_2[1].start()

    @pl.when(jnp.logical_not(even))
    def _():
        pl.semaphore_wait(ok_sem.at[2], 1)

    for present, far, other, way, copies, copies_2 in ways:

        @pl.when(present)
        def _():
            copies[0].start()

        @pl.when(present & seven)
        def _():
            copies_2[0].start()

        @pl.when(present & jnp.logical_not(at_once(lon, far)))
        def _():
            pl.semaphore_signal(
                ok_sem.at[1 - way], inc=1, device_id={"lat": other, "lon": lon}, device_id_type=MESH
            )

    for present, far, other, way, copies, copies_2 in ways:

        @pl.when(present & jnp.logical_not(at_once(lon, far)))
        def _():
            pl.semaphore_wait(ok_sem.at[way], 1)
            copies[1].start()

    key = lax.broadcasted_iota(jnp.int32, (288, 144), 1)
    query = lax.broadcasted_iota(jnp.int32, (288, 144), 0)
    same = lax.rem(key + query, 2) == 0
    for band, known in enumerate(((key >= 72) | has_north, (key >= 72) | has_south)):
        bias[band, 0] = jnp.where(known, 0.0, -1e30)
        bias[band, 1] = jnp.where(known & same, 0.0, -1e30)

    @pl.when(jnp.logical_not(has_north))
    def _():
        halo[:, 0:3] = jnp.zeros((2, 3, 12, 4, D), BF16)

    @pl.when(jnp.logical_not(has_south))
    def _():
        halo[:, 9:12] = jnp.zeros((2, 3, 12, 4, D), BF16)

    def give_back(band):
        return pltpu.make_async_remote_copy(
            src_ref=made.at[0, band, :, 0:6],
            dst_ref=got.at[band],
            send_sem=back_send.at[band],
            recv_sem=back_recv.at[band],
            device_id={"lat": lat, "lon": west},
            device_id_type=MESH,
        )

    for load in loads[:5]:
        load.wait()

    head = lax.div(lax.broadcasted_iota(jnp.int32, (72, 256), 1), HEAD_DIM)
    first = (lat >= middle).astype(jnp.int32)
    windows = 1 + seven.astype(jnp.int32)

    def project(block):
        normed = norm32(flat(block).astype(F32), gain_attn[...])
        return jnp.concatenate(split_levels(normed), axis=0).astype(BF16)

    def own_rows(window):
        @pl.when(window == 0)
        def _():
            to_east.wait_recv()

        @pl.when(window == 1)
        def _():
            to_west.wait_recv()

        tokens = project(halo[window, 3:9])
        for group in range(2):
            rows = tokens[144 * group : 144 * group + 144]
            for part in range(3):
                own[window, group, part] = dot(rows, w_qkv[:, D * part : D * part + D])

    def step(index, carry):
        window, turn = lax.rem(index, windows), lax.div(index, windows)
        band = lax.rem(first + turn, 2)

        @pl.when(turn == 0)
        def _():
            own_rows(window)

        for side, way in ((0, 1), (1, 0)):
            for which in range(2):

                @pl.when((band == side) & ways[side][0] & (window == which))
                def _():
                    for copy in ways[way][4 + which]:
                        copy.wait_recv()

        tokens = project(halo[window, pl.ds(9 * band, 3)])
        others = [dot(tokens, w_qkv[:, D * part : D * part + D]) for part in (1, 2)]
        mixed = []
        for group in range(2):
            rows = slice(72 * group, 72 * group + 72)
            q, k_own, v_own = [own[window, group, part, pl.ds(72 * band, 72)] for part in range(3)]
            q = (q * HEAD_DIM**-0.5).astype(BF16)
            k = jnp.concatenate([others[0][rows], k_own], axis=0).astype(BF16)
            v = jnp.concatenate([others[1][rows], v_own], axis=0).astype(BF16)
            parts = []
            for quad in range(2):
                cols = slice(256 * quad, 256 * quad + 256)
                q_quad = q[:, cols]
                zero = jnp.zeros_like(q_quad)
                stacked = jnp.concatenate([jnp.where(head == h, q_quad, zero) for h in range(4)], axis=0)
                scores = dot_t(stacked, k[:, cols]) + bias[band, group]
                raised = jnp.exp(scores - jnp.max(scores, axis=-1, keepdims=True))
                total = jnp.sum(raised, axis=-1, keepdims=True)
                out = dot(raised.astype(BF16), v[:, cols]) * (1.0 / total)
                part = out[0:72]
                for h in range(1, 4):
                    part = jnp.where(head == h, out[72 * h : 72 * h + 72], part)
                parts.append(part)
            mixed.append(jnp.concatenate(parts, axis=1))
        made[window, band] = join_levels(*mixed).astype(BF16).reshape(3, 12, 4, D)

        @pl.when((window == 0) & jnp.logical_not(eight))
        def _():
            give_back(band).start()

        return carry

    lax.fori_loop(0, 2 * windows, step, 0)

    for load in loads[5:]:
        load.wait()
    early[...] = feed_forward(
        jnp.concatenate([flat(made[0, 0, :, 6:12]), flat(made[0, 1, :, 6:12])], axis=0), xv[:, 0:6], w_out, gain_mlp, w_up, w_down
    )

    @pl.when(seven)
    def _():
        for band in range(2):
            late[3 * band : 3 * band + 3] = made[1, band, :, 0:6]

    @pl.when(jnp.logical_not(seven))
    def _():
        for band in range(2):
            give_back(band).wait_recv()
            late[3 * band : 3 * band + 3] = got[band]

    to_east.wait_send()

    @pl.when(eight)
    def _():
        to_west.wait_send()

    for present, _, _, _, copies, copies_2 in ways:

        @pl.when(present)
        def _():
            for copy in copies:
                copy.wait_send()

        @pl.when(present & seven)
        def _():
            copies_2[0].wait_send()

        @pl.when(present & eight)
        def _():
            copies_2[1].wait_send()

    @pl.when(jnp.logical_not(eight))
    def _():
        give_back(0).wait_send()
        give_back(1).wait_send()


def solution(mesh):
    n_lat, n_lon = mesh.shape["lat"], mesh.shape["lon"]

    def body(tokens, gain_attn, w_qkv, w_out, gain_mlp, w_up, w_down):
        x = tokens.transpose(1, 2, 0, 3)
        gain_attn, gain_mlp = gain_attn.reshape(1, D), gain_mlp.reshape(1, D)
        hbm = pl.BlockSpec(memory_space=pltpu.HBM)
        vmem = pl.BlockSpec(memory_space=pltpu.VMEM)
        held = [
            pltpu.with_memory_space_constraint(a, pltpu.HBM)
            for a in (x, gain_attn, w_qkv, w_out, gain_mlp, w_up, w_down)
        ]
        half = jax.ShapeDtypeStruct((6, 6, 4, D), BF16)
        passed = [jax.ShapeDtypeStruct(a.shape, a.dtype) for a in (x, w_out, gain_mlp, w_up, w_down)]
        made = pl.pallas_call(
            functools.partial(kernel, n_lat, n_lon),
            out_shape=[half, half] + passed,
            in_specs=[hbm] * 7,
            out_specs=[vmem] * 7,
            scratch_shapes=[
                pltpu.VMEM((1, D), F32),
                pltpu.VMEM((2, 12, 12, 4, D), BF16),
                pltpu.VMEM((2, 2, 3, 12, 4, D), BF16),
                pltpu.VMEM((2, 2, 3, 144, D), F32),
                pltpu.VMEM((2, 3, 6, 4, D), BF16),
                pltpu.VMEM((2, 2, 288, 144), F32),
                pltpu.VMEM((D, 3 * D), BF16),
                pltpu.SemaphoreType.DMA((10,)),
                pltpu.SemaphoreType.DMA((10,)),
                pltpu.SemaphoreType.DMA((2,)),
                pltpu.SemaphoreType.DMA((2,)),
                pltpu.SemaphoreType.DMA((6,)),
                pltpu.SemaphoreType.DMA((3,)),
                pltpu.SemaphoreType.REGULAR((3,)),
            ],
            compiler_params=pltpu.CompilerParams(
                collective_id=0, has_side_effects=True, vmem_limit_bytes=40 * 1024 * 1024
            ),
            cost_estimate=pl.CostEstimate(flops=1_800_000_000, bytes_accessed=7_000_000, transcendentals=1_000_000),
        )(*held)
        out = pl.pallas_call(
            finish,
            out_shape=jax.ShapeDtypeStruct(x.shape, BF16),
            in_specs=[vmem] * 7,
            out_specs=hbm,
            scratch_shapes=[pltpu.VMEM((6, 6, 4, D), BF16), pltpu.SemaphoreType.DMA((2,))],
            compiler_params=pltpu.CompilerParams(vmem_limit_bytes=40 * 1024 * 1024),
            cost_estimate=pl.CostEstimate(flops=700_000_000, bytes_accessed=300_000, transcendentals=300_000),
        )(*made)
        return out.transpose(2, 0, 1, 3)

    in_specs = (P(None, "lat", "lon", None), P(), P(), P(), P(), P(), P())
    out_specs = P(None, "lat", "lon", None)
    return jax.shard_map(body, mesh=mesh, in_specs=in_specs, out_specs=out_specs, check_vma=False)
```

```python
import functools

import jax
import jax.numpy as jnp
from jax import lax
from jax.experimental import pallas as pl
from jax.experimental.pallas import tpu as pltpu
from jax.sharding import PartitionSpec as P

HEADS = 8
D = 512
FF = 2048
HEAD_DIM = 64
F32 = jnp.float32
BF16 = jnp.bfloat16
MESH = pl.DeviceIdType.MESH


def norm32(values, gain):
    average = jnp.mean(values, axis=-1, keepdims=True)
    centered = values - average
    spread = jnp.mean(centered * centered, axis=-1, keepdims=True)
    return centered * lax.rsqrt(spread + 1e-05) * gain


def norm(values, gain):
    return norm32(values, gain).astype(BF16)


def inner_levels(shape):
    place = lax.rem(lax.broadcasted_iota(jnp.int32, shape, 1), 4)
    return (place == 1) | (place == 2)


def split_levels(values):
    pairs = values.reshape(values.shape[0] // 16, 2, 8, values.shape[1])
    first, second = pairs[:, 0], pltpu.roll(pairs[:, 1], 2, 1)
    inner = inner_levels(first.shape)
    half = (values.shape[0] // 2, values.shape[1])
    return jnp.where(inner, first, second).reshape(half), jnp.where(inner, second, first).reshape(half)


def join_levels(inner_half, outer_half):
    shape = (inner_half.shape[0] // 8, 8, inner_half.shape[1])
    a, b = inner_half.reshape(shape), outer_half.reshape(shape)
    inner = inner_levels(shape)
    first, second = jnp.where(inner, a, b), pltpu.roll(jnp.where(inner, b, a), 6, 1)
    return jnp.stack([first, second], axis=1).reshape(2 * inner_half.shape[0], inner_half.shape[1])


def flat(block):
    rows = block.shape[0] * block.shape[1] * block.shape[2]
    return block.reshape(rows, block.shape[3])


def gelu(v):
    inner = v * (0.7978845608028654 + 0.035677408136300125 * (v * v))
    return (0.5 * v) * (1.0 + jnp.tanh(inner))


def dot(a, b):
    return jnp.dot(a, b, preferred_element_type=F32)


def dot_t(a, b):
    return lax.dot_general(a, b, (((1,), (1,)), ((), ())), preferred_element_type=F32)


def feed_forward(attended, x, w_out, gain, w_up, w_down):
    residual = (flat(x).astype(F32) + dot(attended, w_out[...])).astype(BF16).astype(F32)
    hidden = gelu(dot(norm(residual, gain[...]), w_up[...])).astype(BF16)
    block = (residual + dot(hidden, w_down[...])).astype(BF16)
    return block.reshape(x.shape)


def finish(n_lon, early, late, xv, w_out, gain, w_up, w_down, o_hbm, done, sem):
    eastern = 6 * (lax.rem(lax.axis_index("lon"), n_lon // 2) == n_lon // 4 - 1).astype(jnp.int32)
    put = pltpu.make_async_copy(early, o_hbm.at[:, pl.ds(eastern, 6)], sem.at[0])
    put.start()
    done[...] = feed_forward(flat(late[...]), xv[:, pl.ds(6 - eastern, 6)], w_out, gain, w_up, w_down)
    last = pltpu.make_async_copy(done, o_hbm.at[:, pl.ds(6 - eastern, 6)], sem.at[1])
    last.start()
    put.wait()
    last.wait()


def kernel(
    n_lat,
    n_lon,
    x_hbm,
    gain_attn_hbm,
    w_qkv_hbm,
    w_out_hbm,
    gain_mlp_hbm,
    w_up_hbm,
    w_down_hbm,
    early,
    late,
    xv,
    w_out,
    gain_mlp,
    w_up,
    w_down,
    gain_attn,
    halo,
    made,
    own,
    got,
    bias,
    w_qkv,
    send_sem,
    recv_sem,
    back_send,
    back_recv,
    w_sem,
    x_sem,
    ok_sem,
):
    lat = lax.axis_index("lat")
    lon = lax.axis_index("lon")
    west = lax.rem(lon + n_lon - 1, n_lon)
    east = lax.rem(lon + 1, n_lon)
    has_north = lat > 0
    has_south = lat < n_lat - 1

    barrier = pltpu.get_barrier_semaphore()

    def greet(la, lo):
        pl.semaphore_signal(barrier, inc=1, device_id={"lat": la, "lon": lo}, device_id_type=MESH)

    middle = n_lat // 2
    far_north, far_south = lat == middle, lat == middle - 1
    even = lax.rem(lon, 2) == 0
    place = lax.rem(lon, n_lon // 2)
    first_place, last_place = place == 0, place == n_lon // 2 - 1
    six, seven, eight = place == n_lon // 4 - 2, place == n_lon // 4 - 1, place == n_lon // 4
    wider, pushes = six | seven, seven | eight
    told = jnp.logical_not(even | last_place)
    greet(lat, west)

    @pl.when(told | six)
    def _():
        greet(lat, east)

    for present, other in ((has_north, lat - 1), (has_south, lat + 1)):

        @pl.when(present & even)
        def _():
            greet(other, lon)

        @pl.when(present & (jnp.logical_not(even) | first_place))
        def _():
            greet(other, west)

        @pl.when(present & wider)
        def _():
            greet(other, east)

    loads = [
        pltpu.make_async_copy(x_hbm, xv, x_sem.at[0]),
        pltpu.make_async_copy(x_hbm.at[:, 0:6], halo.at[0, 3:9, 6:12], x_sem.at[1]),
        pltpu.make_async_copy(x_hbm.at[:, 6:12], halo.at[1, 3:9, 0:6], x_sem.at[2]),
        pltpu.make_async_copy(gain_attn_hbm, gain_attn, w_sem.at[4]),
        pltpu.make_async_copy(w_qkv_hbm, w_qkv, w_sem.at[0]),
        pltpu.make_async_copy(gain_mlp_hbm, gain_mlp, w_sem.at[5]),
        pltpu.make_async_copy(w_out_hbm, w_out, w_sem.at[1]),
        pltpu.make_async_copy(w_up_hbm, w_up, w_sem.at[2]),
        pltpu.make_async_copy(w_down_hbm, w_down, w_sem.at[3]),
    ]
    for load in loads:
        load.start()

    def send(index, src, dst, la, lo):
        return pltpu.make_async_remote_copy(
            src_ref=src,
            dst_ref=dst,
            send_sem=send_sem.at[index],
            recv_sem=recv_sem.at[index],
            device_id={"lat": la, "lon": lo},
            device_id_type=MESH,
        )

    to_east = send(0, x_hbm.at[:, 6:12], halo.at[0, 3:9, 0:6], lat, east)
    to_north = [
        send(1, x_hbm.at[0:3, 0:6], halo.at[0, 9:12, 6:12], lat - 1, lon),
        send(2, x_hbm.at[0:3, 6:12], halo.at[0, 9:12, 0:6], lat - 1, east),
    ]
    to_south = [
        send(3, x_hbm.at[3:6, 0:6], halo.at[0, 0:3, 6:12], lat + 1, lon),
        send(4, x_hbm.at[3:6, 6:12], halo.at[0, 0:3, 0:6], lat + 1, east),
    ]
    to_west = send(5, x_hbm.at[:, 0:6], halo.at[1, 3:9, 6:12], lat, west)
    to_north_2 = [
        send(6, x_hbm.at[0:3, 6:12], halo.at[1, 9:12, 0:6], lat - 1, lon),
        send(7, x_hbm.at[0:3, 0:6], halo.at[1, 9:12, 6:12], lat - 1, west),
    ]
    to_south_2 = [
        send(8, x_hbm.at[3:6, 6:12], halo.at[1, 0:3, 0:6], lat + 1, lon),
        send(9, x_hbm.at[3:6, 0:6], halo.at[1, 0:3, 6:12], lat + 1, west),
    ]

    ways = ((has_north, far_north, to_north, to_north_2), (has_south, far_south, to_south, to_south_2))

    def straight(far):
        for present, is_far, copies, copies_2 in ways:

            @pl.when(present & (is_far == far) & jnp.logical_not(seven))
            def _():
                copies[0].start()

            @pl.when(present & wider & (is_far == far))
            def _():
                copies_2[0].start()

    def corner(far):
        for present, is_far, copies, copies_2 in ways:

            @pl.when(present & (is_far == far) & jnp.logical_not(six))
            def _():
                copies[1].start()

            @pl.when(present & pushes & (is_far == far))
            def _():
                copies_2[1].start()

    greetings = 1 + ((even & jnp.logical_not(first_place)) | seven).astype(jnp.int32)
    for present, *_ in ways:
        for greets in (even, jnp.logical_not(told), pushes):
            greetings += (present & greets).astype(jnp.int32)
    pl.semaphore_wait(barrier, greetings)

    @pl.when(even)
    def _():
        pl.semaphore_signal(ok_sem.at[0], inc=1, device_id={"lat": lat, "lon": east}, device_id_type=MESH)

        @pl.when(jnp.logical_not(first_place))
        def _():
            pl.semaphore_signal(ok_sem.at[1], inc=1, device_id={"lat": lat, "lon": west}, device_id_type=MESH)

        straight(True)
        straight(False)

        @pl.when(jnp.logical_not(six))
        def _():
            to_east.start()

        @pl.when(eight)
        def _():
            to_west.start()

        corner(True)
        corner(False)

    @pl.when(last_place)
    def _():
        to_east.start()
        corner(True)
        corner(False)
        pl.semaphore_wait(ok_sem.at[0], 1)
        straight(False)
        straight(True)

    @pl.when(told)
    def _():
        to_east.start()

        @pl.when(seven)
        def _():
            to_west.start()

        pl.semaphore_wait(ok_sem.at[0], 1)
        straight(False)
        pl.semaphore_wait(ok_sem.at[1], 1)
        corner(True)
        corner(False)
        straight(True)

    key = lax.broadcasted_iota(jnp.int32, (144, 144), 1)
    query = lax.broadcasted_iota(jnp.int32, (144, 144), 0)
    same = lax.rem(key + query, 2) == 0
    for band, known in enumerate(((key >= 72) | has_north, (key >= 72) | has_south)):
        bias[band, 0] = jnp.where(known, 0.0, -1e30)
        bias[band, 1] = jnp.where(known & same, 0.0, -1e30)

    @pl.when(jnp.logical_not(has_north))
    def _():
        halo[:, 0:3] = jnp.zeros((2, 3, 12, 4, D), BF16)

    @pl.when(jnp.logical_not(has_south))
    def _():
        halo[:, 9:12] = jnp.zeros((2, 3, 12, 4, D), BF16)

    def give_back(band):
        return pltpu.make_async_remote_copy(
            src_ref=made.at[0, band, :, 0:6],
            dst_ref=got.at[band],
            send_sem=back_send.at[band],
            recv_sem=back_recv.at[band],
            device_id={"lat": lat, "lon": west},
            device_id_type=MESH,
        )

    def give_on(band):
        return pltpu.make_async_remote_copy(
            src_ref=made.at[1, band, :, 6:12],
            dst_ref=got.at[band],
            send_sem=back_send.at[2 + band],
            recv_sem=back_recv.at[band],
            device_id={"lat": lat, "lon": east},
            device_id_type=MESH,
        )

    for load in loads[:5]:
        load.wait()

    low = lax.broadcasted_iota(jnp.int32, (72, 128), 1) < HEAD_DIM
    first = (lat >= middle).astype(jnp.int32)
    only = seven.astype(jnp.int32)
    middle_rows = far_north | far_south

    def project(block):
        normed = norm32(flat(block).astype(F32), gain_attn[...])
        return jnp.concatenate(split_levels(normed), axis=0).astype(BF16)

    def own_rows(window):
        @pl.when(window == 0)
        def _():
            to_east.wait_recv()

        @pl.when(window == 1)
        def _():
            to_west.wait_recv()

        tokens = project(halo[window, 3:9])
        for group in range(2):
            rows = tokens[144 * group : 144 * group + 144]
            for part in range(3):
                own[window, group, part] = dot(rows, w_qkv[:, D * part : D * part + D])

    def step(window, turn):
        band = lax.rem(first + turn, 2)

        @pl.when(turn == 0)
        def _():
            own_rows(window)

        for side, way in ((0, 1), (1, 0)):
            for which in range(2):

                @pl.when((band == side) & ways[side][0] & (window == which))
                def _():
                    for copy in ways[way][2 + which]:
                        copy.wait_recv()

        tokens = project(halo[window, pl.ds(9 * band, 3)])
        others = [dot(tokens, w_qkv[:, D * part : D * part + D]) for part in (1, 2)]
        mixed = []
        for group in range(2):
            rows = slice(72 * group, 72 * group + 72)
            q, k_own, v_own = [own[window, group, part, pl.ds(72 * band, 72)] for part in range(3)]
            q = (q * HEAD_DIM**-0.5).astype(BF16)
            k = jnp.concatenate([others[0][rows], k_own], axis=0).astype(BF16)
            v = jnp.concatenate([others[1][rows], v_own], axis=0).astype(BF16)
            parts = []
            for pair in range(HEADS // 2):
                cols = slice(128 * pair, 128 * pair + 128)
                q_pair = q[:, cols]
                zero = jnp.zeros_like(q_pair)
                stacked = jnp.concatenate([jnp.where(low, q_pair, zero), jnp.where(low, zero, q_pair)], axis=0)
                scores = dot_t(stacked, k[:, cols]) + bias[band, group]
                raised = jnp.exp(scores - jnp.max(scores, axis=-1, keepdims=True))
                total = jnp.sum(raised, axis=-1, keepdims=True)
                out = dot(raised.astype(BF16), v[:, cols]) * (1.0 / total)
                parts.append(jnp.where(low, out[0:72], out[72:144]))
            mixed.append(jnp.concatenate(parts, axis=1))
        made[window, band] = join_levels(*mixed).astype(BF16).reshape(3, 12, 4, D)

        @pl.when((window == 0) & jnp.logical_not(eight))
        def _():
            give_back(band).start()

        @pl.when((window == 1) & six)
        def _():
            give_on(band).start()

    step(only, 0)

    @pl.when(six & middle_rows)
    def _():
        step(1, 0)

    step(only, 1)

    @pl.when(six)
    def _():
        lax.fori_loop(middle_rows.astype(jnp.int32), 2, lambda turn, carry: (step(1, turn), carry)[1], 0)

    for load in loads[5:]:
        load.wait()
    kept = 6 * (1 - only)
    early[...] = feed_forward(
        jnp.concatenate([flat(made[only, band, :, pl.ds(kept, 6)]) for band in range(2)], axis=0),
        xv[:, pl.ds(6 * only, 6)],
        w_out,
        gain_mlp,
        w_up,
        w_down,
    )

    @pl.when(six)
    def _():
        for band in range(2):
            late[3 * band : 3 * band + 3] = made[1, band, :, 0:6]

    @pl.when(jnp.logical_not(six))
    def _():
        for band in range(2):
            give_back(band).wait_recv()
            late[3 * band : 3 * band + 3] = got[band]

    def sent(condition, copy):
        @pl.when(condition)
        def _():
            copy.wait_send()

    sent(jnp.logical_not(six), to_east)
    sent(pushes, to_west)
    for present, _, copies, copies_2 in ways:
        sent(present & jnp.logical_not(seven), copies[0])
        sent(present & jnp.logical_not(six), copies[1])
        sent(present & wider, copies_2[0])
        sent(present & pushes, copies_2[1])
    for band in range(2):
        sent(jnp.logical_not(pushes), give_back(band))
        sent(six, give_on(band))


def solution(mesh):
    n_lat, n_lon = mesh.shape["lat"], mesh.shape["lon"]

    def body(tokens, gain_attn, w_qkv, w_out, gain_mlp, w_up, w_down):
        x = tokens.transpose(1, 2, 0, 3)
        gain_attn, gain_mlp = gain_attn.reshape(1, D), gain_mlp.reshape(1, D)
        hbm = pl.BlockSpec(memory_space=pltpu.HBM)
        vmem = pl.BlockSpec(memory_space=pltpu.VMEM)
        held = [
            pltpu.with_memory_space_constraint(a, pltpu.HBM)
            for a in (x, gain_attn, w_qkv, w_out, gain_mlp, w_up, w_down)
        ]
        half = jax.ShapeDtypeStruct((6, 6, 4, D), BF16)
        passed = [jax.ShapeDtypeStruct(a.shape, a.dtype) for a in (x, w_out, gain_mlp, w_up, w_down)]
        made = pl.pallas_call(
            functools.partial(kernel, n_lat, n_lon),
            out_shape=[half, half] + passed,
            in_specs=[hbm] * 7,
            out_specs=[vmem] * 7,
            scratch_shapes=[
                pltpu.VMEM((1, D), F32),
                pltpu.VMEM((2, 12, 12, 4, D), BF16),
                pltpu.VMEM((2, 2, 3, 12, 4, D), BF16),
                pltpu.VMEM((2, 2, 3, 144, D), F32),
                pltpu.VMEM((2, 3, 6, 4, D), BF16),
                pltpu.VMEM((2, 2, 144, 144), F32),
                pltpu.VMEM((D, 3 * D), BF16),
                pltpu.SemaphoreType.DMA((10,)),
                pltpu.SemaphoreType.DMA((10,)),
                pltpu.SemaphoreType.DMA((4,)),
                pltpu.SemaphoreType.DMA((2,)),
                pltpu.SemaphoreType.DMA((6,)),
                pltpu.SemaphoreType.DMA((3,)),
                pltpu.SemaphoreType.REGULAR((2,)),
            ],
            compiler_params=pltpu.CompilerParams(
                collective_id=0, has_side_effects=True, vmem_limit_bytes=40 * 1024 * 1024
            ),
            cost_estimate=pl.CostEstimate(flops=1_800_000_000, bytes_accessed=7_000_000, transcendentals=1_000_000),
        )(*held)
        out = pl.pallas_call(
            functools.partial(finish, n_lon),
            out_shape=jax.ShapeDtypeStruct(x.shape, BF16),
            in_specs=[vmem] * 7,
            out_specs=hbm,
            scratch_shapes=[pltpu.VMEM((6, 6, 4, D), BF16), pltpu.SemaphoreType.DMA((2,))],
            compiler_params=pltpu.CompilerParams(vmem_limit_bytes=40 * 1024 * 1024),
            cost_estimate=pl.CostEstimate(flops=700_000_000, bytes_accessed=300_000, transcendentals=300_000),
        )(*made)
        return out.transpose(2, 0, 1, 3)

    in_specs = (P(None, "lat", "lon", None), P(), P(), P(), P(), P(), P())
    out_specs = P(None, "lat", "lon", None)
    return jax.shard_map(body, mesh=mesh, in_specs=in_specs, out_specs=out_specs, check_vma=False)
```

```python
import functools

import jax
import jax.numpy as jnp
from jax import lax
from jax.experimental import pallas as pl
from jax.experimental.pallas import tpu as pltpu
from jax.sharding import PartitionSpec as P

HEADS = 8
D = 512
FF = 2048
HEAD_DIM = 64
F32 = jnp.float32
BF16 = jnp.bfloat16
MESH = pl.DeviceIdType.MESH


def norm32(values, gain):
    average = jnp.mean(values, axis=-1, keepdims=True)
    centered = values - average
    spread = jnp.mean(centered * centered, axis=-1, keepdims=True)
    return centered * lax.rsqrt(spread + 1e-05) * gain


def norm(values, gain):
    return norm32(values, gain).astype(BF16)


def inner_levels(shape):
    place = lax.rem(lax.broadcasted_iota(jnp.int32, shape, 1), 4)
    return (place == 1) | (place == 2)


def split_levels(values):
    pairs = values.reshape(values.shape[0] // 16, 2, 8, values.shape[1])
    first, second = pairs[:, 0], pltpu.roll(pairs[:, 1], 2, 1)
    inner = inner_levels(first.shape)
    half = (values.shape[0] // 2, values.shape[1])
    return jnp.where(inner, first, second).reshape(half), jnp.where(inner, second, first).reshape(half)


def join_levels(inner_half, outer_half):
    shape = (inner_half.shape[0] // 8, 8, inner_half.shape[1])
    a, b = inner_half.reshape(shape), outer_half.reshape(shape)
    inner = inner_levels(shape)
    first, second = jnp.where(inner, a, b), pltpu.roll(jnp.where(inner, b, a), 6, 1)
    return jnp.stack([first, second], axis=1).reshape(2 * inner_half.shape[0], inner_half.shape[1])


def flat(block):
    rows = block.shape[0] * block.shape[1] * block.shape[2]
    return block.reshape(rows, block.shape[3])


def gelu(v):
    inner = v * (0.7978845608028654 + 0.035677408136300125 * (v * v))
    return (0.5 * v) * (1.0 + jnp.tanh(inner))


def dot(a, b):
    return jnp.dot(a, b, preferred_element_type=F32)


def dot_t(a, b):
    return lax.dot_general(a, b, (((1,), (1,)), ((), ())), preferred_element_type=F32)


def feed_forward(attended, x, w_out, gain, w_up, w_down):
    residual = (flat(x).astype(F32) + dot(attended, w_out[...])).astype(BF16).astype(F32)
    hidden = gelu(dot(norm(residual, gain[...]), w_up[...])).astype(BF16)
    block = (residual + dot(hidden, w_down[...])).astype(BF16)
    return block.reshape(x.shape)


def finish(n_lon, early, late, xv, w_out, gain, w_up, w_down, o_hbm, done, sem):
    place = lax.rem(lax.axis_index("lon"), n_lon // 2)
    eastern = 6 * (place == n_lon // 4 - 1).astype(jnp.int32)
    whole = place == 0
    put = pltpu.make_async_copy(early, o_hbm.at[:, pl.ds(eastern, 6)], sem.at[0])
    put.start()

    def last(src):
        return pltpu.make_async_copy(src, o_hbm.at[:, pl.ds(6 - eastern, 6)], sem.at[1])

    @pl.when(whole)
    def _():
        last(late).start()

    @pl.when(jnp.logical_not(whole))
    def _():
        done[...] = feed_forward(flat(late[...]), xv[:, pl.ds(6 - eastern, 6)], w_out, gain, w_up, w_down)
        last(done).start()

    put.wait()
    last(done).wait()


def kernel(
    n_lat,
    n_lon,
    x_hbm,
    gain_attn_hbm,
    w_qkv_hbm,
    w_out_hbm,
    gain_mlp_hbm,
    w_up_hbm,
    w_down_hbm,
    early,
    late,
    xv,
    w_out,
    gain_mlp,
    w_up,
    w_down,
    gain_attn,
    halo,
    made,
    own,
    got,
    bias,
    w_qkv,
    send_sem,
    recv_sem,
    back_send,
    back_recv,
    w_sem,
    x_sem,
    ok_sem,
):
    lat = lax.axis_index("lat")
    lon = lax.axis_index("lon")
    west = lax.rem(lon + n_lon - 1, n_lon)
    east = lax.rem(lon + 1, n_lon)
    has_north = lat > 0
    has_south = lat < n_lat - 1

    barrier = pltpu.get_barrier_semaphore()

    def greet(la, lo):
        pl.semaphore_signal(barrier, inc=1, device_id={"lat": la, "lon": lo}, device_id_type=MESH)

    middle = n_lat // 2
    far_north, far_south = lat == middle, lat == middle - 1
    even = lax.rem(lon, 2) == 0
    place = lax.rem(lon, n_lon // 2)
    first_place, last_place = place == 0, place == n_lon // 2 - 1
    six, seven, eight = place == n_lon // 4 - 2, place == n_lon // 4 - 1, place == n_lon // 4
    wider, pushes = six | seven, seven | eight
    told = jnp.logical_not(even | last_place)
    greet(lat, west)

    @pl.when(told | six)
    def _():
        greet(lat, east)

    for present, other in ((has_north, lat - 1), (has_south, lat + 1)):

        @pl.when(present & even)
        def _():
            greet(other, lon)

        @pl.when(present & (jnp.logical_not(even) | first_place))
        def _():
            greet(other, west)

        @pl.when(present & wider)
        def _():
            greet(other, east)

    loads = [
        pltpu.make_async_copy(x_hbm, xv, x_sem.at[0]),
        pltpu.make_async_copy(x_hbm.at[:, 0:6], halo.at[0, 3:9, 6:12], x_sem.at[1]),
        pltpu.make_async_copy(x_hbm.at[:, 6:12], halo.at[1, 3:9, 0:6], x_sem.at[2]),
        pltpu.make_async_copy(gain_attn_hbm, gain_attn, w_sem.at[4]),
        pltpu.make_async_copy(w_qkv_hbm, w_qkv, w_sem.at[0]),
        pltpu.make_async_copy(gain_mlp_hbm, gain_mlp, w_sem.at[5]),
        pltpu.make_async_copy(w_out_hbm, w_out, w_sem.at[1]),
        pltpu.make_async_copy(w_up_hbm, w_up, w_sem.at[2]),
        pltpu.make_async_copy(w_down_hbm, w_down, w_sem.at[3]),
    ]
    for load in loads:
        load.start()

    def send(index, src, dst, la, lo):
        return pltpu.make_async_remote_copy(
            src_ref=src,
            dst_ref=dst,
            send_sem=send_sem.at[index],
            recv_sem=recv_sem.at[index],
            device_id={"lat": la, "lon": lo},
            device_id_type=MESH,
        )

    to_east = send(0, x_hbm.at[:, 6:12], halo.at[0, 3:9, 0:6], lat, east)
    to_north = [
        send(1, x_hbm.at[0:3, 0:6], halo.at[0, 9:12, 6:12], lat - 1, lon),
        send(2, x_hbm.at[0:3, 6:12], halo.at[0, 9:12, 0:6], lat - 1, east),
    ]
    to_south = [
        send(3, x_hbm.at[3:6, 0:6], halo.at[0, 0:3, 6:12], lat + 1, lon),
        send(4, x_hbm.at[3:6, 6:12], halo.at[0, 0:3, 0:6], lat + 1, east),
    ]
    to_west = send(5, x_hbm.at[:, 0:6], halo.at[1, 3:9, 6:12], lat, west)
    to_north_2 = [
        send(6, x_hbm.at[0:3, 6:12], halo.at[1, 9:12, 0:6], lat - 1, lon),
        send(7, x_hbm.at[0:3, 0:6], halo.at[1, 9:12, 6:12], lat - 1, west),
    ]
    to_south_2 = [
        send(8, x_hbm.at[3:6, 6:12], halo.at[1, 0:3, 0:6], lat + 1, lon),
        send(9, x_hbm.at[3:6, 0:6], halo.at[1, 0:3, 6:12], lat + 1, west),
    ]

    ways = ((has_north, far_north, to_north, to_north_2), (has_south, far_south, to_south, to_south_2))

    def straight(far):
        for present, is_far, copies, copies_2 in ways:

            @pl.when(present & (is_far == far) & jnp.logical_not(seven))
            def _():
                copies[0].start()

            @pl.when(present & wider & (is_far == far))
            def _():
                copies_2[0].start()

    def corner(far):
        for present, is_far, copies, copies_2 in ways:

            @pl.when(present & (is_far == far) & jnp.logical_not(six))
            def _():
                copies[1].start()

            @pl.when(present & pushes & (is_far == far))
            def _():
                copies_2[1].start()

    greetings = 1 + ((even & jnp.logical_not(first_place)) | seven).astype(jnp.int32)
    for present, *_ in ways:
        for greets in (even, jnp.logical_not(told), pushes):
            greetings += (present & greets).astype(jnp.int32)
    pl.semaphore_wait(barrier, greetings)

    @pl.when(even)
    def _():
        pl.semaphore_signal(ok_sem.at[0], inc=1, device_id={"lat": lat, "lon": east}, device_id_type=MESH)

        @pl.when(jnp.logical_not(first_place))
        def _():
            pl.semaphore_signal(ok_sem.at[1], inc=1, device_id={"lat": lat, "lon": west}, device_id_type=MESH)

        @pl.when(first_place)
        def _():
            corner(True)

        @pl.when(jnp.logical_not(first_place))
        def _():
            straight(True)

        straight(False)

        @pl.when(jnp.logical_not(six))
        def _():
            to_east.start()

        @pl.when(eight)
        def _():
            to_west.start()

        @pl.when(jnp.logical_not(first_place))
        def _():
            corner(True)

        corner(False)

        @pl.when(first_place)
        def _():
            straight(True)

    @pl.when(last_place)
    def _():
        to_east.start()
        corner(True)
        corner(False)
        pl.semaphore_wait(ok_sem.at[0], 1)
        straight(False)
        straight(True)

    @pl.when(told)
    def _():
        to_east.start()

        @pl.when(seven)
        def _():
            to_west.start()

        pl.semaphore_wait(ok_sem.at[0], 1)

        @pl.when(place == 1)
        def _():
            straight(True)

        straight(False)
        pl.semaphore_wait(ok_sem.at[1], 1)
        corner(True)
        corner(False)

        @pl.when(place != 1)
        def _():
            straight(True)

    key = lax.broadcasted_iota(jnp.int32, (144, 144), 1)
    query = lax.broadcasted_iota(jnp.int32, (144, 144), 0)
    same = lax.rem(key + query, 2) == 0
    for band, known in enumerate(((key >= 72) | has_north, (key >= 72) | has_south)):
        bias[band, 0] = jnp.where(known, 0.0, -1e30)
        bias[band, 1] = jnp.where(known & same, 0.0, -1e30)

    @pl.when(jnp.logical_not(has_north))
    def _():
        halo[:, 0:3] = jnp.zeros((2, 3, 12, 4, D), BF16)

    @pl.when(jnp.logical_not(has_south))
    def _():
        halo[:, 9:12] = jnp.zeros((2, 3, 12, 4, D), BF16)

    def give_back(band):
        return pltpu.make_async_remote_copy(
            src_ref=made.at[0, band, :, 0:6],
            dst_ref=got.at[band],
            send_sem=back_send.at[band],
            recv_sem=back_recv.at[band],
            device_id={"lat": lat, "lon": west},
            device_id_type=MESH,
        )

    def give_on(band):
        return pltpu.make_async_remote_copy(
            src_ref=made.at[1, band, :, 6:12],
            dst_ref=got.at[band],
            send_sem=back_send.at[2 + band],
            recv_sem=back_recv.at[band],
            device_id={"lat": lat, "lon": east},
            device_id_type=MESH,
        )

    for load in loads:
        load.wait()

    low = lax.broadcasted_iota(jnp.int32, (72, 128), 1) < HEAD_DIM
    first = (lat >= middle).astype(jnp.int32)
    only = seven.astype(jnp.int32)

    def project(block):
        normed = norm32(flat(block).astype(F32), gain_attn[...])
        return jnp.concatenate(split_levels(normed), axis=0).astype(BF16)

    def own_rows(window):
        @pl.when(window == 0)
        def _():
            to_east.wait_recv()

        @pl.when(window == 1)
        def _():
            to_west.wait_recv()

        tokens = project(halo[window, 3:9])
        for group in range(2):
            rows = tokens[144 * group : 144 * group + 144]
            for part in range(3):
                own[window, group, part] = dot(rows, w_qkv[:, D * part : D * part + D])

    def step(window, turn):
        band = lax.rem(first + turn, 2)

        @pl.when((turn == 0) & ((window == 0) | seven))
        def _():
            own_rows(window)

        for side, way in ((0, 1), (1, 0)):
            for which in range(2):

                @pl.when((band == side) & ways[side][0] & (window == which))
                def _():
                    for copy in ways[way][2 + which]:
                        copy.wait_recv()

        tokens = project(halo[window, pl.ds(9 * band, 3)])
        others = [dot(tokens, w_qkv[:, D * part : D * part + D]) for part in (1, 2)]
        mixed = []
        for group in range(2):
            rows = slice(72 * group, 72 * group + 72)
            q, k_own, v_own = [own[window, group, part, pl.ds(72 * band, 72)] for part in range(3)]
            q = (q * HEAD_DIM**-0.5).astype(BF16)
            k = jnp.concatenate([others[0][rows], k_own], axis=0).astype(BF16)
            v = jnp.concatenate([others[1][rows], v_own], axis=0).astype(BF16)
            parts = []
            for pair in range(HEADS // 2):
                cols = slice(128 * pair, 128 * pair + 128)
                q_pair = q[:, cols]
                zero = jnp.zeros_like(q_pair)
                stacked = jnp.concatenate([jnp.where(low, q_pair, zero), jnp.where(low, zero, q_pair)], axis=0)
                scores = dot_t(stacked, k[:, cols]) + bias[band, group]
                raised = jnp.exp(scores - jnp.max(scores, axis=-1, keepdims=True))
                total = jnp.sum(raised, axis=-1, keepdims=True)
                out = dot(raised.astype(BF16), v[:, cols]) * (1.0 / total)
                parts.append(jnp.where(low, out[0:72], out[72:144]))
            mixed.append(jnp.concatenate(parts, axis=1))
        made[window, band] = join_levels(*mixed).astype(BF16).reshape(3, 12, 4, D)

        @pl.when((window == 0) & jnp.logical_not(eight))
        def _():
            give_back(band).start()

        @pl.when((window == 1) & six)
        def _():
            give_on(band).start()

    step(only, 0)

    @pl.when(six)
    def _():
        own_rows(1)

    step(only, 1)

    @pl.when(six)
    def _():
        lax.fori_loop(0, 2, lambda turn, carry: (step(1, turn), carry)[1], 0)

    kept = 6 * (1 - only)
    early[...] = feed_forward(
        jnp.concatenate([flat(made[only, band, :, pl.ds(kept, 6)]) for band in range(2)], axis=0),
        xv[:, pl.ds(6 * only, 6)],
        w_out,
        gain_mlp,
        w_up,
        w_down,
    )

    @pl.when(six)
    def _():
        for band in range(2):
            late[3 * band : 3 * band + 3] = made[1, band, :, 0:6]

    @pl.when(jnp.logical_not(six))
    def _():
        for band in range(2):
            give_back(band).wait_recv()

    @pl.when(jnp.logical_not(six | first_place))
    def _():
        for band in range(2):
            late[3 * band : 3 * band + 3] = got[band]

    @pl.when(first_place)
    def _():
        late[...] = feed_forward(
            jnp.concatenate([flat(got[0]), flat(got[1])], axis=0), xv[:, 6:12], w_out, gain_mlp, w_up, w_down
        )

    def sent(condition, copy):
        @pl.when(condition)
        def _():
            copy.wait_send()

    sent(jnp.logical_not(six), to_east)
    sent(pushes, to_west)
    for present, _, copies, copies_2 in ways:
        sent(present & jnp.logical_not(seven), copies[0])
        sent(present & jnp.logical_not(six), copies[1])
        sent(present & wider, copies_2[0])
        sent(present & pushes, copies_2[1])
    for band in range(2):
        sent(jnp.logical_not(pushes), give_back(band))
        sent(six, give_on(band))


def solution(mesh):
    n_lat, n_lon = mesh.shape["lat"], mesh.shape["lon"]

    def body(tokens, gain_attn, w_qkv, w_out, gain_mlp, w_up, w_down):
        x = tokens.transpose(1, 2, 0, 3)
        gain_attn, gain_mlp = gain_attn.reshape(1, D), gain_mlp.reshape(1, D)
        hbm = pl.BlockSpec(memory_space=pltpu.HBM)
        vmem = pl.BlockSpec(memory_space=pltpu.VMEM)
        held = [
            pltpu.with_memory_space_constraint(a, pltpu.HBM)
            for a in (x, gain_attn, w_qkv, w_out, gain_mlp, w_up, w_down)
        ]
        half = jax.ShapeDtypeStruct((6, 6, 4, D), BF16)
        passed = [jax.ShapeDtypeStruct(a.shape, a.dtype) for a in (x, w_out, gain_mlp, w_up, w_down)]
        made = pl.pallas_call(
            functools.partial(kernel, n_lat, n_lon),
            out_shape=[half, half] + passed,
            in_specs=[hbm] * 7,
            out_specs=[vmem] * 7,
            scratch_shapes=[
                pltpu.VMEM((1, D), F32),
                pltpu.VMEM((2, 12, 12, 4, D), BF16),
                pltpu.VMEM((2, 2, 3, 12, 4, D), BF16),
                pltpu.VMEM((2, 2, 3, 144, D), F32),
                pltpu.VMEM((2, 3, 6, 4, D), BF16),
                pltpu.VMEM((2, 2, 144, 144), F32),
                pltpu.VMEM((D, 3 * D), BF16),
                pltpu.SemaphoreType.DMA((10,)),
                pltpu.SemaphoreType.DMA((10,)),
                pltpu.SemaphoreType.DMA((4,)),
                pltpu.SemaphoreType.DMA((2,)),
                pltpu.SemaphoreType.DMA((6,)),
                pltpu.SemaphoreType.DMA((3,)),
                pltpu.SemaphoreType.REGULAR((2,)),
            ],
            compiler_params=pltpu.CompilerParams(
                collective_id=0, has_side_effects=True, vmem_limit_bytes=40 * 1024 * 1024
            ),
            cost_estimate=pl.CostEstimate(flops=1_800_000_000, bytes_accessed=7_000_000, transcendentals=1_000_000),
        )(*held)
        out = pl.pallas_call(
            functools.partial(finish, n_lon),
            out_shape=jax.ShapeDtypeStruct(x.shape, BF16),
            in_specs=[vmem] * 7,
            out_specs=hbm,
            scratch_shapes=[pltpu.VMEM((6, 6, 4, D), BF16), pltpu.SemaphoreType.DMA((2,))],
            compiler_params=pltpu.CompilerParams(vmem_limit_bytes=40 * 1024 * 1024),
            cost_estimate=pl.CostEstimate(flops=700_000_000, bytes_accessed=300_000, transcendentals=300_000),
        )(*made)
        return out.transpose(2, 0, 1, 3)

    in_specs = (P(None, "lat", "lon", None), P(), P(), P(), P(), P(), P())
    out_specs = P(None, "lat", "lon", None)
    return jax.shard_map(body, mesh=mesh, in_specs=in_specs, out_specs=out_specs, check_vma=False)
```

```python
import functools

import jax
import jax.numpy as jnp
from jax import lax
from jax.experimental import pallas as pl
from jax.experimental.pallas import tpu as pltpu
from jax.sharding import PartitionSpec as P

HEADS = 8
D = 512
FF = 2048
HEAD_DIM = 64
F32 = jnp.float32
BF16 = jnp.bfloat16
MESH = pl.DeviceIdType.MESH


def norm32(values, gain):
    average = jnp.mean(values, axis=-1, keepdims=True)
    centered = values - average
    spread = jnp.mean(centered * centered, axis=-1, keepdims=True)
    return centered * lax.rsqrt(spread + 1e-05) * gain


def norm(values, gain):
    return norm32(values, gain).astype(BF16)


def inner_levels(shape):
    place = lax.rem(lax.broadcasted_iota(jnp.int32, shape, 1), 4)
    return (place == 1) | (place == 2)


def split_levels(values):
    pairs = values.reshape(values.shape[0] // 16, 2, 8, values.shape[1])
    first, second = pairs[:, 0], pltpu.roll(pairs[:, 1], 2, 1)
    inner = inner_levels(first.shape)
    half = (values.shape[0] // 2, values.shape[1])
    return jnp.where(inner, first, second).reshape(half), jnp.where(inner, second, first).reshape(half)


def join_levels(inner_half, outer_half):
    shape = (inner_half.shape[0] // 8, 8, inner_half.shape[1])
    a, b = inner_half.reshape(shape), outer_half.reshape(shape)
    inner = inner_levels(shape)
    first, second = jnp.where(inner, a, b), pltpu.roll(jnp.where(inner, b, a), 6, 1)
    return jnp.stack([first, second], axis=1).reshape(2 * inner_half.shape[0], inner_half.shape[1])


def flat(block):
    rows = block.shape[0] * block.shape[1] * block.shape[2]
    return block.reshape(rows, block.shape[3])


def gelu(v):
    inner = v * (0.7978845608028654 + 0.035677408136300125 * (v * v))
    return (0.5 * v) * (1.0 + jnp.tanh(inner))


def dot(a, b):
    return jnp.dot(a, b, preferred_element_type=F32)


def dot_t(a, b):
    return lax.dot_general(a, b, (((1,), (1,)), ((), ())), preferred_element_type=F32)


def feed_forward(attended, x, w_out, gain, w_up, w_down):
    residual = (flat(x).astype(F32) + dot(attended, w_out[...])).astype(BF16).astype(F32)
    hidden = gelu(dot(norm(residual, gain[...]), w_up[...])).astype(BF16)
    block = (residual + dot(hidden, w_down[...])).astype(BF16)
    return block.reshape(x.shape)


def finish(n_lon, early, late, xv, w_out, gain, w_up, w_down, o_hbm, done, sem):
    place = lax.rem(lax.axis_index("lon"), n_lon // 2)
    eastern = 6 * (place == n_lon // 4 - 1).astype(jnp.int32)
    whole = place == 0
    put = pltpu.make_async_copy(early, o_hbm.at[:, pl.ds(eastern, 6)], sem.at[0])
    put.start()

    def last(src):
        return pltpu.make_async_copy(src, o_hbm.at[:, pl.ds(6 - eastern, 6)], sem.at[1])

    @pl.when(whole)
    def _():
        last(late).start()

    @pl.when(jnp.logical_not(whole))
    def _():
        done[...] = feed_forward(flat(late[...]), xv[:, pl.ds(6 - eastern, 6)], w_out, gain, w_up, w_down)
        last(done).start()

    put.wait()
    last(done).wait()


def kernel(
    n_lat,
    n_lon,
    x_hbm,
    gain_attn_hbm,
    w_qkv_hbm,
    w_out_hbm,
    gain_mlp_hbm,
    w_up_hbm,
    w_down_hbm,
    early,
    late,
    xv,
    w_out,
    gain_mlp,
    w_up,
    w_down,
    gain_attn,
    halo,
    made,
    own,
    got,
    bias,
    w_qkv,
    send_sem,
    recv_sem,
    back_send,
    back_recv,
    w_sem,
    x_sem,
    ok_sem,
):
    lat = lax.axis_index("lat")
    lon = lax.axis_index("lon")
    west = lax.rem(lon + n_lon - 1, n_lon)
    east = lax.rem(lon + 1, n_lon)
    has_north = lat > 0
    has_south = lat < n_lat - 1

    barrier = pltpu.get_barrier_semaphore()

    def greet(la, lo):
        pl.semaphore_signal(barrier, inc=1, device_id={"lat": la, "lon": lo}, device_id_type=MESH)

    middle = n_lat // 2
    far_north, far_south = lat == middle, lat == middle - 1
    even = lax.rem(lon, 2) == 0
    place = lax.rem(lon, n_lon // 2)
    first_place, last_place = place == 0, place == n_lon // 2 - 1
    six, seven, eight = place == n_lon // 4 - 2, place == n_lon // 4 - 1, place == n_lon // 4
    wider, pushes = six | seven, seven | eight
    told = jnp.logical_not(even | last_place)
    greet(lat, west)

    @pl.when(told | six)
    def _():
        greet(lat, east)

    for present, other in ((has_north, lat - 1), (has_south, lat + 1)):

        @pl.when(present & even)
        def _():
            greet(other, lon)

        @pl.when(present & (jnp.logical_not(even) | first_place))
        def _():
            greet(other, west)

        @pl.when(present & wider)
        def _():
            greet(other, east)

    loads = [
        pltpu.make_async_copy(x_hbm, xv, x_sem.at[0]),
        pltpu.make_async_copy(x_hbm.at[:, 0:6], halo.at[0, 3:9, 6:12], x_sem.at[1]),
        pltpu.make_async_copy(x_hbm.at[:, 6:12], halo.at[1, 3:9, 0:6], x_sem.at[2]),
        pltpu.make_async_copy(gain_attn_hbm, gain_attn, w_sem.at[4]),
        pltpu.make_async_copy(w_qkv_hbm, w_qkv, w_sem.at[0]),
        pltpu.make_async_copy(gain_mlp_hbm, gain_mlp, w_sem.at[5]),
        pltpu.make_async_copy(w_out_hbm, w_out, w_sem.at[1]),
        pltpu.make_async_copy(w_up_hbm, w_up, w_sem.at[2]),
        pltpu.make_async_copy(w_down_hbm, w_down, w_sem.at[3]),
    ]
    for load in loads:
        load.start()

    def send(index, src, dst, la, lo):
        return pltpu.make_async_remote_copy(
            src_ref=src,
            dst_ref=dst,
            send_sem=send_sem.at[index],
            recv_sem=recv_sem.at[index],
            device_id={"lat": la, "lon": lo},
            device_id_type=MESH,
        )

    to_east = send(0, x_hbm.at[:, 6:12], halo.at[0, 3:9, 0:6], lat, east)
    to_north = [
        send(1, x_hbm.at[0:3, 0:6], halo.at[0, 9:12, 6:12], lat - 1, lon),
        send(2, x_hbm.at[0:3, 6:12], halo.at[0, 9:12, 0:6], lat - 1, east),
    ]
    to_south = [
        send(3, x_hbm.at[3:6, 0:6], halo.at[0, 0:3, 6:12], lat + 1, lon),
        send(4, x_hbm.at[3:6, 6:12], halo.at[0, 0:3, 0:6], lat + 1, east),
    ]
    to_west = send(5, x_hbm.at[:, 0:6], halo.at[1, 3:9, 6:12], lat, west)
    to_north_2 = [
        send(6, x_hbm.at[0:3, 6:12], halo.at[1, 9:12, 0:6], lat - 1, lon),
        send(7, x_hbm.at[0:3, 0:6], halo.at[1, 9:12, 6:12], lat - 1, west),
    ]
    to_south_2 = [
        send(8, x_hbm.at[3:6, 6:12], halo.at[1, 0:3, 0:6], lat + 1, lon),
        send(9, x_hbm.at[3:6, 0:6], halo.at[1, 0:3, 6:12], lat + 1, west),
    ]

    ways = ((has_north, far_north, to_north, to_north_2), (has_south, far_south, to_south, to_south_2))

    def straight(far):
        for present, is_far, copies, copies_2 in ways:

            @pl.when(present & (is_far == far) & jnp.logical_not(seven))
            def _():
                copies[0].start()

            @pl.when(present & wider & (is_far == far))
            def _():
                copies_2[0].start()

    def corner(far):
        for present, is_far, copies, copies_2 in ways:

            @pl.when(present & pushes & (is_far == far))
            def _():
                copies_2[1].start()

            @pl.when(present & (is_far == far) & jnp.logical_not(six))
            def _():
                copies[1].start()

    greetings = 1 + ((even & jnp.logical_not(first_place)) | seven).astype(jnp.int32)
    for present, *_ in ways:
        for greets in (even, jnp.logical_not(told), pushes):
            greetings += (present & greets).astype(jnp.int32)
    pl.semaphore_wait(barrier, greetings)

    @pl.when(even)
    def _():
        pl.semaphore_signal(ok_sem.at[0], inc=1, device_id={"lat": lat, "lon": east}, device_id_type=MESH)

        @pl.when(jnp.logical_not(first_place))
        def _():
            pl.semaphore_signal(ok_sem.at[1], inc=1, device_id={"lat": lat, "lon": west}, device_id_type=MESH)

        @pl.when(eight)
        def _():
            to_west.start()

        @pl.when(first_place)
        def _():
            corner(True)

        @pl.when(jnp.logical_not(first_place))
        def _():
            straight(True)

        straight(False)

        @pl.when(jnp.logical_not(six))
        def _():
            to_east.start()

        @pl.when(jnp.logical_not(first_place))
        def _():
            corner(True)

        corner(False)

        @pl.when(first_place)
        def _():
            straight(True)

    @pl.when(last_place)
    def _():
        to_east.start()
        corner(True)
        corner(False)
        pl.semaphore_wait(ok_sem.at[0], 1)
        straight(False)
        straight(True)

    @pl.when(told)
    def _():
        to_east.start()

        @pl.when(seven)
        def _():
            to_west.start()

        pl.semaphore_wait(ok_sem.at[0], 1)

        @pl.when(place == 1)
        def _():
            straight(True)

        straight(False)
        pl.semaphore_wait(ok_sem.at[1], 1)
        corner(True)
        corner(False)

        @pl.when(place != 1)
        def _():
            straight(True)

    key = lax.broadcasted_iota(jnp.int32, (144, 144), 1)
    query = lax.broadcasted_iota(jnp.int32, (144, 144), 0)
    same = lax.rem(key + query, 2) == 0
    for band, known in enumerate(((key >= 72) | has_north, (key >= 72) | has_south)):
        bias[band, 0] = jnp.where(known, 0.0, -1e30)
        bias[band, 1] = jnp.where(known & same, 0.0, -1e30)

    @pl.when(jnp.logical_not(has_north))
    def _():
        halo[:, 0:3] = jnp.zeros((2, 3, 12, 4, D), BF16)

    @pl.when(jnp.logical_not(has_south))
    def _():
        halo[:, 9:12] = jnp.zeros((2, 3, 12, 4, D), BF16)

    def give_back(band):
        return pltpu.make_async_remote_copy(
            src_ref=made.at[0, band, :, 0:6],
            dst_ref=got.at[band],
            send_sem=back_send.at[band],
            recv_sem=back_recv.at[band],
            device_id={"lat": lat, "lon": west},
            device_id_type=MESH,
        )

    def give_on(band):
        return pltpu.make_async_remote_copy(
            src_ref=made.at[1, band, :, 6:12],
            dst_ref=got.at[band],
            send_sem=back_send.at[2 + band],
            recv_sem=back_recv.at[band],
            device_id={"lat": lat, "lon": east},
            device_id_type=MESH,
        )

    for load in loads:
        load.wait()

    low = lax.broadcasted_iota(jnp.int32, (72, 128), 1) < HEAD_DIM
    first = (lat >= middle).astype(jnp.int32)
    only = seven.astype(jnp.int32)

    def project(block):
        normed = norm32(flat(block).astype(F32), gain_attn[...])
        return jnp.concatenate(split_levels(normed), axis=0).astype(BF16)

    def own_rows(window):
        @pl.when(window == 0)
        def _():
            to_east.wait_recv()

        @pl.when(window == 1)
        def _():
            to_west.wait_recv()

        tokens = project(halo[window, 3:9])
        for group in range(2):
            rows = tokens[144 * group : 144 * group + 144]
            for part in range(3):
                own[window, group, part] = dot(rows, w_qkv[:, D * part : D * part + D])

    def step(window, turn):
        band = lax.rem(first + turn, 2)

        @pl.when((turn == 0) & ((window == 0) | seven))
        def _():
            own_rows(window)

        for side, way in ((0, 1), (1, 0)):
            for which in range(2):

                @pl.when((band == side) & ways[side][0] & (window == which))
                def _():
                    for copy in ways[way][2 + which]:
                        copy.wait_recv()

        tokens = project(halo[window, pl.ds(9 * band, 3)])
        others = [dot(tokens, w_qkv[:, D * part : D * part + D]) for part in (1, 2)]
        mixed = []
        for group in range(2):
            rows = slice(72 * group, 72 * group + 72)
            q, k_own, v_own = [own[window, group, part, pl.ds(72 * band, 72)] for part in range(3)]
            q = (q * HEAD_DIM**-0.5).astype(BF16)
            k = jnp.concatenate([others[0][rows], k_own], axis=0).astype(BF16)
            v = jnp.concatenate([others[1][rows], v_own], axis=0).astype(BF16)
            parts = []
            for pair in range(HEADS // 2):
                cols = slice(128 * pair, 128 * pair + 128)
                q_pair = q[:, cols]
                zero = jnp.zeros_like(q_pair)
                stacked = jnp.concatenate([jnp.where(low, q_pair, zero), jnp.where(low, zero, q_pair)], axis=0)
                scores = dot_t(stacked, k[:, cols]) + bias[band, group]
                raised = jnp.exp(scores - jnp.max(scores, axis=-1, keepdims=True))
                total = jnp.sum(raised, axis=-1, keepdims=True)
                out = dot(raised.astype(BF16), v[:, cols]) * (1.0 / total)
                parts.append(jnp.where(low, out[0:72], out[72:144]))
            mixed.append(jnp.concatenate(parts, axis=1))
        made[window, band] = join_levels(*mixed).astype(BF16).reshape(3, 12, 4, D)

        @pl.when((window == 0) & jnp.logical_not(eight))
        def _():
            give_back(band).start()

        @pl.when((window == 1) & six)
        def _():
            give_on(band).start()

    step(only, 0)

    @pl.when(six)
    def _():
        own_rows(1)

    step(only, 1)

    @pl.when(six)
    def _():
        lax.fori_loop(0, 2, lambda turn, carry: (step(1, turn), carry)[1], 0)

    kept = 6 * (1 - only)
    early[...] = feed_forward(
        jnp.concatenate([flat(made[only, band, :, pl.ds(kept, 6)]) for band in range(2)], axis=0),
        xv[:, pl.ds(6 * only, 6)],
        w_out,
        gain_mlp,
        w_up,
        w_down,
    )

    def sent(condition, copy):
        @pl.when(condition)
        def _():
            copy.wait_send()

    sent(jnp.logical_not(six), to_east)
    sent(pushes, to_west)
    for present, _, copies, copies_2 in ways:
        sent(present & jnp.logical_not(seven), copies[0])
        sent(present & jnp.logical_not(six), copies[1])
        sent(present & wider, copies_2[0])
        sent(present & pushes, copies_2[1])
    for band in range(2):
        sent(jnp.logical_not(pushes | first_place), give_back(band))
        sent(six, give_on(band))

    @pl.when(six)
    def _():
        for band in range(2):
            late[3 * band : 3 * band + 3] = made[1, band, :, 0:6]

    @pl.when(jnp.logical_not(six))
    def _():
        for band in range(2):
            give_back(band).wait_recv()

    @pl.when(jnp.logical_not(six | first_place))
    def _():
        for band in range(2):
            late[3 * band : 3 * band + 3] = got[band]

    @pl.when(first_place)
    def _():
        late[...] = feed_forward(
            jnp.concatenate([flat(got[0]), flat(got[1])], axis=0), xv[:, 6:12], w_out, gain_mlp, w_up, w_down
        )

    for band in range(2):
        sent(first_place, give_back(band))


def solution(mesh):
    n_lat, n_lon = mesh.shape["lat"], mesh.shape["lon"]

    def body(tokens, gain_attn, w_qkv, w_out, gain_mlp, w_up, w_down):
        x = tokens.transpose(1, 2, 0, 3)
        gain_attn, gain_mlp = gain_attn.reshape(1, D), gain_mlp.reshape(1, D)
        hbm = pl.BlockSpec(memory_space=pltpu.HBM)
        vmem = pl.BlockSpec(memory_space=pltpu.VMEM)
        held = [
            pltpu.with_memory_space_constraint(a, pltpu.HBM)
            for a in (x, gain_attn, w_qkv, w_out, gain_mlp, w_up, w_down)
        ]
        half = jax.ShapeDtypeStruct((6, 6, 4, D), BF16)
        passed = [jax.ShapeDtypeStruct(a.shape, a.dtype) for a in (x, w_out, gain_mlp, w_up, w_down)]
        made = pl.pallas_call(
            functools.partial(kernel, n_lat, n_lon),
            out_shape=[half, half] + passed,
            in_specs=[hbm] * 7,
            out_specs=[vmem] * 7,
            scratch_shapes=[
                pltpu.VMEM((1, D), F32),
                pltpu.VMEM((2, 12, 12, 4, D), BF16),
                pltpu.VMEM((2, 2, 3, 12, 4, D), BF16),
                pltpu.VMEM((2, 2, 3, 144, D), F32),
                pltpu.VMEM((2, 3, 6, 4, D), BF16),
                pltpu.VMEM((2, 2, 144, 144), F32),
                pltpu.VMEM((D, 3 * D), BF16),
                pltpu.SemaphoreType.DMA((10,)),
                pltpu.SemaphoreType.DMA((10,)),
                pltpu.SemaphoreType.DMA((4,)),
                pltpu.SemaphoreType.DMA((2,)),
                pltpu.SemaphoreType.DMA((6,)),
                pltpu.SemaphoreType.DMA((3,)),
                pltpu.SemaphoreType.REGULAR((2,)),
            ],
            compiler_params=pltpu.CompilerParams(
                collective_id=0, has_side_effects=True, vmem_limit_bytes=40 * 1024 * 1024
            ),
            cost_estimate=pl.CostEstimate(flops=1_800_000_000, bytes_accessed=7_000_000, transcendentals=1_000_000),
        )(*held)
        out = pl.pallas_call(
            functools.partial(finish, n_lon),
            out_shape=jax.ShapeDtypeStruct(x.shape, BF16),
            in_specs=[vmem] * 7,
            out_specs=hbm,
            scratch_shapes=[pltpu.VMEM((6, 6, 4, D), BF16), pltpu.SemaphoreType.DMA((2,))],
            compiler_params=pltpu.CompilerParams(vmem_limit_bytes=40 * 1024 * 1024),
            cost_estimate=pl.CostEstimate(flops=700_000_000, bytes_accessed=300_000, transcendentals=300_000),
        )(*made)
        return out.transpose(2, 0, 1, 3)

    in_specs = (P(None, "lat", "lon", None), P(), P(), P(), P(), P(), P())
    out_specs = P(None, "lat", "lon", None)
    return jax.shard_map(body, mesh=mesh, in_specs=in_specs, out_specs=out_specs, check_vma=False)
```

```python
import functools

import jax
import jax.numpy as jnp
from jax import lax
from jax.experimental import pallas as pl
from jax.experimental.pallas import tpu as pltpu
from jax.sharding import PartitionSpec as P

HEADS = 8
D = 512
FF = 2048
HEAD_DIM = 64
F32 = jnp.float32
BF16 = jnp.bfloat16
MESH = pl.DeviceIdType.MESH


def norm32(values, gain):
    average = jnp.mean(values, axis=-1, keepdims=True)
    centered = values - average
    spread = jnp.mean(centered * centered, axis=-1, keepdims=True)
    return centered * lax.rsqrt(spread + 1e-05) * gain


def norm(values, gain):
    return norm32(values, gain).astype(BF16)


def inner_levels(shape):
    place = lax.rem(lax.broadcasted_iota(jnp.int32, shape, 1), 4)
    return (place == 1) | (place == 2)


def split_levels(values):
    pairs = values.reshape(values.shape[0] // 16, 2, 8, values.shape[1])
    first, second = pairs[:, 0], pltpu.roll(pairs[:, 1], 2, 1)
    inner = inner_levels(first.shape)
    half = (values.shape[0] // 2, values.shape[1])
    return jnp.where(inner, first, second).reshape(half), jnp.where(inner, second, first).reshape(half)


def join_levels(inner_half, outer_half):
    shape = (inner_half.shape[0] // 8, 8, inner_half.shape[1])
    a, b = inner_half.reshape(shape), outer_half.reshape(shape)
    inner = inner_levels(shape)
    first, second = jnp.where(inner, a, b), pltpu.roll(jnp.where(inner, b, a), 6, 1)
    return jnp.stack([first, second], axis=1).reshape(2 * inner_half.shape[0], inner_half.shape[1])


def flat(block):
    rows = block.shape[0] * block.shape[1] * block.shape[2]
    return block.reshape(rows, block.shape[3])


def gelu(v):
    inner = v * (0.7978845608028654 + 0.035677408136300125 * (v * v))
    return (0.5 * v) * (1.0 + jnp.tanh(inner))


def dot(a, b):
    return jnp.dot(a, b, preferred_element_type=F32)


def dot_t(a, b):
    return lax.dot_general(a, b, (((1,), (1,)), ((), ())), preferred_element_type=F32)


def feed_forward(attended, x, w_out, gain, w_up, w_down):
    residual = (x.astype(F32) + dot(attended, w_out[...])).astype(BF16).astype(F32)
    hidden = gelu(dot(norm(residual, gain[...]), w_up[...])).astype(BF16)
    return (residual + dot(hidden, w_down[...])).astype(BF16)


def has_whole(lon, n_lon):
    place = lax.rem(lon, n_lon // 2)
    return (place == 0) | (place == n_lon // 4 - 1)


def finish(n_lon, early, late, xv, w_out, gain, w_up, w_down, o_hbm, done, sem):
    whole = has_whole(lax.axis_index("lon"), n_lon)
    put = pltpu.make_async_copy(early, o_hbm.at[:, 0:6], sem.at[0])
    put.start()

    def last(src):
        return pltpu.make_async_copy(src, o_hbm.at[:, 6:12], sem.at[1])

    @pl.when(whole)
    def _():
        last(late).start()

    @pl.when(jnp.logical_not(whole))
    def _():
        done[...] = feed_forward(flat(late[...]), flat(xv[:, 6:12]), w_out, gain, w_up, w_down).reshape(done.shape)
        last(done).start()

    put.wait()
    last(done).wait()


def kernel(
    n_lat,
    n_lon,
    x_hbm,
    gain_attn_hbm,
    w_qkv_hbm,
    w_out_hbm,
    gain_mlp_hbm,
    w_up_hbm,
    w_down_hbm,
    early,
    late,
    xv,
    w_out,
    gain_mlp,
    w_up,
    w_down,
    gain_attn,
    halo,
    made,
    own,
    got,
    bias,
    w_qkv,
    send_sem,
    recv_sem,
    back_send,
    back_recv,
    w_sem,
    x_sem,
    ok_sem,
):
    lat = lax.axis_index("lat")
    lon = lax.axis_index("lon")
    west = lax.rem(lon + n_lon - 1, n_lon)
    east = lax.rem(lon + 1, n_lon)
    has_north = lat > 0
    has_south = lat < n_lat - 1

    barrier = pltpu.get_barrier_semaphore()

    def greet(la, lo):
        pl.semaphore_signal(barrier, inc=1, device_id={"lat": la, "lon": lo}, device_id_type=MESH)

    middle = n_lat // 2
    far_north, far_south = lat == middle, lat == middle - 1
    even = lax.rem(lon, 2) == 0
    place = lax.rem(lon, n_lon // 2)
    first_place, last_place = place == 0, place == n_lon // 2 - 1
    six, seven, eight = place == n_lon // 4 - 2, place == n_lon // 4 - 1, place == n_lon // 4
    wider, pushes = six | seven, seven | eight
    told = jnp.logical_not(even | last_place)
    greet(lat, west)

    @pl.when(told | six)
    def _():
        greet(lat, east)

    for present, other in ((has_north, lat - 1), (has_south, lat + 1)):

        @pl.when(present & even)
        def _():
            greet(other, lon)

        @pl.when(present & (jnp.logical_not(even) | first_place))
        def _():
            greet(other, west)

        @pl.when(present & wider)
        def _():
            greet(other, east)

    loads = [
        pltpu.make_async_copy(x_hbm, xv, x_sem.at[0]),
        pltpu.make_async_copy(x_hbm.at[:, 0:6], halo.at[0, 3:9, 6:12], x_sem.at[1]),
        pltpu.make_async_copy(x_hbm.at[:, 6:12], halo.at[1, 3:9, 0:6], x_sem.at[2]),
        pltpu.make_async_copy(gain_attn_hbm, gain_attn, w_sem.at[4]),
        pltpu.make_async_copy(w_qkv_hbm, w_qkv, w_sem.at[0]),
        pltpu.make_async_copy(gain_mlp_hbm, gain_mlp, w_sem.at[5]),
        pltpu.make_async_copy(w_out_hbm, w_out, w_sem.at[1]),
        pltpu.make_async_copy(w_up_hbm, w_up, w_sem.at[2]),
        pltpu.make_async_copy(w_down_hbm, w_down, w_sem.at[3]),
    ]
    for load in loads:
        load.start()

    def send(index, src, dst, la, lo):
        return pltpu.make_async_remote_copy(
            src_ref=src,
            dst_ref=dst,
            send_sem=send_sem.at[index],
            recv_sem=recv_sem.at[index],
            device_id={"lat": la, "lon": lo},
            device_id_type=MESH,
        )

    to_east = send(0, x_hbm.at[:, 6:12], halo.at[0, 3:9, 0:6], lat, east)
    to_north = [
        send(1, x_hbm.at[0:3, 0:6], halo.at[0, 9:12, 6:12], lat - 1, lon),
        send(2, x_hbm.at[0:3, 6:12], halo.at[0, 9:12, 0:6], lat - 1, east),
    ]
    to_south = [
        send(3, x_hbm.at[3:6, 0:6], halo.at[0, 0:3, 6:12], lat + 1, lon),
        send(4, x_hbm.at[3:6, 6:12], halo.at[0, 0:3, 0:6], lat + 1, east),
    ]
    to_west = send(5, x_hbm.at[:, 0:6], halo.at[1, 3:9, 6:12], lat, west)
    to_north_2 = [
        send(6, x_hbm.at[0:3, 6:12], halo.at[1, 9:12, 0:6], lat - 1, lon),
        send(7, x_hbm.at[0:3, 0:6], halo.at[1, 9:12, 6:12], lat - 1, west),
    ]
    to_south_2 = [
        send(8, x_hbm.at[3:6, 6:12], halo.at[1, 0:3, 0:6], lat + 1, lon),
        send(9, x_hbm.at[3:6, 0:6], halo.at[1, 0:3, 6:12], lat + 1, west),
    ]

    ways = ((has_north, far_north, to_north, to_north_2), (has_south, far_south, to_south, to_south_2))

    def straight(far):
        for present, is_far, copies, copies_2 in ways:

            @pl.when(present & (is_far == far) & jnp.logical_not(seven))
            def _():
                copies[0].start()

            @pl.when(present & wider & (is_far == far))
            def _():
                copies_2[0].start()

    def corner(far):
        for present, is_far, copies, copies_2 in ways:

            @pl.when(present & pushes & (is_far == far))
            def _():
                copies_2[1].start()

            @pl.when(present & (is_far == far) & jnp.logical_not(six))
            def _():
                copies[1].start()

    greetings = 1 + ((even & jnp.logical_not(first_place)) | seven).astype(jnp.int32)
    for present, *_ in ways:
        for greets in (even, jnp.logical_not(told), pushes):
            greetings += (present & greets).astype(jnp.int32)
    pl.semaphore_wait(barrier, greetings)

    @pl.when(even)
    def _():
        pl.semaphore_signal(ok_sem.at[0], inc=1, device_id={"lat": lat, "lon": east}, device_id_type=MESH)

        @pl.when(jnp.logical_not(first_place))
        def _():
            pl.semaphore_signal(ok_sem.at[1], inc=1, device_id={"lat": lat, "lon": west}, device_id_type=MESH)

        @pl.when(eight)
        def _():
            to_west.start()

        @pl.when(first_place)
        def _():
            corner(True)

        @pl.when(jnp.logical_not(first_place))
        def _():
            straight(True)

        straight(False)

        @pl.when(jnp.logical_not(six))
        def _():
            to_east.start()

        @pl.when(jnp.logical_not(first_place))
        def _():
            corner(True)

        corner(False)

        @pl.when(first_place)
        def _():
            straight(True)

    @pl.when(last_place)
    def _():
        to_east.start()
        corner(True)
        corner(False)
        pl.semaphore_wait(ok_sem.at[0], 1)
        straight(False)
        straight(True)

    @pl.when(told)
    def _():
        to_east.start()

        @pl.when(seven)
        def _():
            to_west.start()

        pl.semaphore_wait(ok_sem.at[0], 1)

        @pl.when(place == 1)
        def _():
            straight(True)

        straight(False)
        pl.semaphore_wait(ok_sem.at[1], 1)
        corner(True)
        corner(False)

        @pl.when(place != 1)
        def _():
            straight(True)

    key = lax.broadcasted_iota(jnp.int32, (144, 144), 1)
    query = lax.broadcasted_iota(jnp.int32, (144, 144), 0)
    same = lax.rem(key + query, 2) == 0
    for band, known in enumerate(((key >= 72) | has_north, (key >= 72) | has_south)):
        bias[band, 0] = jnp.where(known, 0.0, -1e30)
        bias[band, 1] = jnp.where(known & same, 0.0, -1e30)

    @pl.when(jnp.logical_not(has_north))
    def _():
        halo[:, 0:3] = jnp.zeros((2, 3, 12, 4, D), BF16)

    @pl.when(jnp.logical_not(has_south))
    def _():
        halo[:, 9:12] = jnp.zeros((2, 3, 12, 4, D), BF16)

    def give_back(band):
        return pltpu.make_async_remote_copy(
            src_ref=made.at[0, band, :, 0:6],
            dst_ref=got.at[band],
            send_sem=back_send.at[band],
            recv_sem=back_recv.at[band],
            device_id={"lat": lat, "lon": west},
            device_id_type=MESH,
        )

    def give_on(band):
        return pltpu.make_async_remote_copy(
            src_ref=made.at[1, band, :, 6:12],
            dst_ref=got.at[band],
            send_sem=back_send.at[2 + band],
            recv_sem=back_recv.at[band],
            device_id={"lat": lat, "lon": east},
            device_id_type=MESH,
        )

    for load in loads:
        load.wait()

    low = lax.broadcasted_iota(jnp.int32, (72, 128), 1) < HEAD_DIM
    first = (lat >= middle).astype(jnp.int32)
    only = seven.astype(jnp.int32)

    def project(block):
        normed = norm32(flat(block).astype(F32), gain_attn[...])
        return jnp.concatenate(split_levels(normed), axis=0).astype(BF16)

    def own_rows(window):
        @pl.when(window == 0)
        def _():
            to_east.wait_recv()

        @pl.when(window == 1)
        def _():
            to_west.wait_recv()

        tokens = project(halo[window, 3:9])
        for group in range(2):
            rows = tokens[144 * group : 144 * group + 144]
            for part in range(3):
                own[window, group, part] = dot(rows, w_qkv[:, D * part : D * part + D])

    def step(window, turn):
        band = lax.rem(first + turn, 2)

        @pl.when((turn == 0) & ((window == 0) | seven))
        def _():
            own_rows(window)

        for side, way in ((0, 1), (1, 0)):
            for which in range(2):

                @pl.when((band == side) & ways[side][0] & (window == which))
                def _():
                    for copy in ways[way][2 + which]:
                        copy.wait_recv()

        tokens = project(halo[window, pl.ds(9 * band, 3)])
        others = [dot(tokens, w_qkv[:, D * part : D * part + D]) for part in (1, 2)]
        mixed = []
        for group in range(2):
            rows = slice(72 * group, 72 * group + 72)
            q, k_own, v_own = [own[window, group, part, pl.ds(72 * band, 72)] for part in range(3)]
            q = (q * HEAD_DIM**-0.5).astype(BF16)
            k = jnp.concatenate([others[0][rows], k_own], axis=0).astype(BF16)
            v = jnp.concatenate([others[1][rows], v_own], axis=0).astype(BF16)
            parts = []
            for pair in range(HEADS // 2):
                cols = slice(128 * pair, 128 * pair + 128)
                q_pair = q[:, cols]
                zero = jnp.zeros_like(q_pair)
                stacked = jnp.concatenate([jnp.where(low, q_pair, zero), jnp.where(low, zero, q_pair)], axis=0)
                scores = dot_t(stacked, k[:, cols]) + bias[band, group]
                raised = jnp.exp(scores - jnp.max(scores, axis=-1, keepdims=True))
                total = jnp.sum(raised, axis=-1, keepdims=True)
                out = dot(raised.astype(BF16), v[:, cols]) * (1.0 / total)
                parts.append(jnp.where(low, out[0:72], out[72:144]))
            mixed.append(jnp.concatenate(parts, axis=1))
        made[window, band] = join_levels(*mixed).astype(BF16).reshape(3, 12, 4, D)

        @pl.when((window == 0) & jnp.logical_not(eight))
        def _():
            give_back(band).start()

        @pl.when((window == 1) & six)
        def _():
            give_on(band).start()

    step(only, 0)

    @pl.when(six)
    def _():
        own_rows(1)

    step(only, 1)

    @pl.when(six)
    def _():
        lax.fori_loop(0, 2, lambda turn, carry: (step(1, turn), carry)[1], 0)

    whole = has_whole(lon, n_lon)

    @pl.when(jnp.logical_not(whole))
    def _():
        attended = jnp.concatenate([flat(made[0, band, :, 6:12]) for band in range(2)], axis=0)
        early[...] = feed_forward(attended, flat(xv[:, 0:6]), w_out, gain_mlp, w_up, w_down).reshape(early.shape)

    def sent(condition, copy):
        @pl.when(condition)
        def _():
            copy.wait_send()

    sent(jnp.logical_not(six), to_east)
    sent(pushes, to_west)
    for present, _, copies, copies_2 in ways:
        sent(present & jnp.logical_not(seven), copies[0])
        sent(present & jnp.logical_not(six), copies[1])
        sent(present & wider, copies_2[0])
        sent(present & pushes, copies_2[1])
    for band in range(2):
        sent(jnp.logical_not(pushes | first_place), give_back(band))
        sent(six, give_on(band))

    @pl.when(six)
    def _():
        for band in range(2):
            late[3 * band : 3 * band + 3] = made[1, band, :, 0:6]

    @pl.when(jnp.logical_not(six))
    def _():
        for band in range(2):
            give_back(band).wait_recv()

    @pl.when(jnp.logical_not(six | seven))
    def _():
        for band in range(2):
            late[3 * band : 3 * band + 3] = got[band]

    @pl.when(first_place)
    def _():
        for band in range(2):
            early[3 * band : 3 * band + 3] = made[0, band, :, 6:12]

    @pl.when(seven)
    def _():
        for band in range(2):
            early[3 * band : 3 * band + 3] = got[band]
            late[3 * band : 3 * band + 3] = made[1, band, :, 0:6]

    @pl.when(whole)
    def _():
        attended = jnp.concatenate([flat(early[...]), flat(late[...])], axis=0)
        x = jnp.concatenate([flat(xv[:, 0:6]), flat(xv[:, 6:12])], axis=0)
        values = feed_forward(attended, x, w_out, gain_mlp, w_up, w_down)
        early[...] = values[0:144].reshape(early.shape)
        late[...] = values[144:288].reshape(late.shape)

    for band in range(2):
        sent(first_place, give_back(band))


def solution(mesh):
    n_lat, n_lon = mesh.shape["lat"], mesh.shape["lon"]

    def body(tokens, gain_attn, w_qkv, w_out, gain_mlp, w_up, w_down):
        x = tokens.transpose(1, 2, 0, 3)
        gain_attn, gain_mlp = gain_attn.reshape(1, D), gain_mlp.reshape(1, D)
        hbm = pl.BlockSpec(memory_space=pltpu.HBM)
        vmem = pl.BlockSpec(memory_space=pltpu.VMEM)
        held = [
            pltpu.with_memory_space_constraint(a, pltpu.HBM)
            for a in (x, gain_attn, w_qkv, w_out, gain_mlp, w_up, w_down)
        ]
        half = jax.ShapeDtypeStruct((6, 6, 4, D), BF16)
        passed = [jax.ShapeDtypeStruct(a.shape, a.dtype) for a in (x, w_out, gain_mlp, w_up, w_down)]
        made = pl.pallas_call(
            functools.partial(kernel, n_lat, n_lon),
            out_shape=[half, half] + passed,
            in_specs=[hbm] * 7,
            out_specs=[vmem] * 7,
            scratch_shapes=[
                pltpu.VMEM((1, D), F32),
                pltpu.VMEM((2, 12, 12, 4, D), BF16),
                pltpu.VMEM((2, 2, 3, 12, 4, D), BF16),
                pltpu.VMEM((2, 2, 3, 144, D), F32),
                pltpu.VMEM((2, 3, 6, 4, D), BF16),
                pltpu.VMEM((2, 2, 144, 144), F32),
                pltpu.VMEM((D, 3 * D), BF16),
                pltpu.SemaphoreType.DMA((10,)),
                pltpu.SemaphoreType.DMA((10,)),
                pltpu.SemaphoreType.DMA((4,)),
                pltpu.SemaphoreType.DMA((2,)),
                pltpu.SemaphoreType.DMA((6,)),
                pltpu.SemaphoreType.DMA((3,)),
                pltpu.SemaphoreType.REGULAR((2,)),
            ],
            compiler_params=pltpu.CompilerParams(
                collective_id=0, has_side_effects=True, vmem_limit_bytes=40 * 1024 * 1024
            ),
            cost_estimate=pl.CostEstimate(flops=1_800_000_000, bytes_accessed=7_000_000, transcendentals=1_000_000),
        )(*held)
        out = pl.pallas_call(
            functools.partial(finish, n_lon),
            out_shape=jax.ShapeDtypeStruct(x.shape, BF16),
            in_specs=[vmem] * 7,
            out_specs=hbm,
            scratch_shapes=[pltpu.VMEM((6, 6, 4, D), BF16), pltpu.SemaphoreType.DMA((2,))],
            compiler_params=pltpu.CompilerParams(vmem_limit_bytes=40 * 1024 * 1024),
            cost_estimate=pl.CostEstimate(flops=700_000_000, bytes_accessed=300_000, transcendentals=300_000),
        )(*made)
        return out.transpose(2, 0, 1, 3)

    in_specs = (P(None, "lat", "lon", None), P(), P(), P(), P(), P(), P())
    out_specs = P(None, "lat", "lon", None)
    return jax.shard_map(body, mesh=mesh, in_specs=in_specs, out_specs=out_specs, check_vma=False)
```

```python
import functools

import jax
import jax.numpy as jnp
from jax import lax
from jax.experimental import pallas as pl
from jax.experimental.pallas import tpu as pltpu
from jax.sharding import PartitionSpec as P

HEADS = 8
D = 512
FF = 2048
HEAD_DIM = 64
F32 = jnp.float32
BF16 = jnp.bfloat16
MESH = pl.DeviceIdType.MESH


def norm32(values, gain):
    average = jnp.mean(values, axis=-1, keepdims=True)
    centered = values - average
    spread = jnp.mean(centered * centered, axis=-1, keepdims=True)
    return centered * lax.rsqrt(spread + 1e-05) * gain


def norm(values, gain):
    return norm32(values, gain).astype(BF16)


def inner_levels(shape):
    place = lax.rem(lax.broadcasted_iota(jnp.int32, shape, 1), 4)
    return (place == 1) | (place == 2)


def split_levels(values):
    pairs = values.reshape(values.shape[0] // 16, 2, 8, values.shape[1])
    first, second = pairs[:, 0], pltpu.roll(pairs[:, 1], 2, 1)
    inner = inner_levels(first.shape)
    half = (values.shape[0] // 2, values.shape[1])
    return jnp.where(inner, first, second).reshape(half), jnp.where(inner, second, first).reshape(half)


def join_levels(inner_half, outer_half):
    shape = (inner_half.shape[0] // 8, 8, inner_half.shape[1])
    a, b = inner_half.reshape(shape), outer_half.reshape(shape)
    inner = inner_levels(shape)
    first, second = jnp.where(inner, a, b), pltpu.roll(jnp.where(inner, b, a), 6, 1)
    return jnp.stack([first, second], axis=1).reshape(2 * inner_half.shape[0], inner_half.shape[1])


def flat(block):
    rows = block.shape[0] * block.shape[1] * block.shape[2]
    return block.reshape(rows, block.shape[3])


def gelu(v):
    inner = v * (0.7978845608028654 + 0.035677408136300125 * (v * v))
    return (0.5 * v) * (1.0 + jnp.tanh(inner))


def dot(a, b):
    return jnp.dot(a, b, preferred_element_type=F32)


def dot_t(a, b):
    return lax.dot_general(a, b, (((1,), (1,)), ((), ())), preferred_element_type=F32)


def feed_forward(attended, x, w_out, gain, w_up, w_down):
    residual = (x.astype(F32) + dot(attended, w_out[...])).astype(BF16).astype(F32)
    hidden = gelu(dot(norm(residual, gain[...]), w_up[...])).astype(BF16)
    return (residual + dot(hidden, w_down[...])).astype(BF16)


def has_whole(lon, n_lon):
    place = lax.rem(lon, n_lon // 2)
    return (place == 0) | (place == n_lon // 4 - 1)


def finish(n_lon, early, late, xv, w_out, gain, w_up, w_down, o_hbm, done, sem):
    whole = has_whole(lax.axis_index("lon"), n_lon)
    put = pltpu.make_async_copy(early, o_hbm.at[:, 0:6], sem.at[0])
    put.start()

    def last(src):
        return pltpu.make_async_copy(src, o_hbm.at[:, 6:12], sem.at[1])

    @pl.when(whole)
    def _():
        last(late).start()

    @pl.when(jnp.logical_not(whole))
    def _():
        done[...] = feed_forward(flat(late[...]), flat(xv[:, 6:12]), w_out, gain, w_up, w_down).reshape(done.shape)
        last(done).start()

    put.wait()
    last(done).wait()


def kernel(
    n_lat,
    n_lon,
    x_hbm,
    gain_attn_hbm,
    w_qkv_hbm,
    w_out_hbm,
    gain_mlp_hbm,
    w_up_hbm,
    w_down_hbm,
    early,
    late,
    xv,
    w_out,
    gain_mlp,
    w_up,
    w_down,
    gain_attn,
    halo,
    made,
    own,
    got,
    bias,
    w_qkv,
    send_sem,
    recv_sem,
    back_send,
    back_recv,
    w_sem,
    x_sem,
    ok_sem,
):
    lat = lax.axis_index("lat")
    lon = lax.axis_index("lon")
    west = lax.rem(lon + n_lon - 1, n_lon)
    east = lax.rem(lon + 1, n_lon)
    north = lax.rem(lat + n_lat - 1, n_lat)
    south = lax.rem(lat + 1, n_lat)
    has_north = lat > 0
    has_south = lat < n_lat - 1

    barrier = pltpu.get_barrier_semaphore()

    def greet(la, lo):
        pl.semaphore_signal(barrier, inc=1, device_id={"lat": la, "lon": lo}, device_id_type=MESH)

    middle = n_lat // 2
    far_north, far_south = lat == middle, lat == middle - 1
    even = lax.rem(lon, 2) == 0
    place = lax.rem(lon, n_lon // 2)
    first_place, last_place = place == 0, place == n_lon // 2 - 1
    six, seven, eight = place == n_lon // 4 - 2, place == n_lon // 4 - 1, place == n_lon // 4
    wider, pushes = six | seven, seven | eight
    told = jnp.logical_not(even | last_place)
    greet(lat, west)

    @pl.when(told | six)
    def _():
        greet(lat, east)

    for present, other in ((has_north, north), (has_south, south)):

        @pl.when(present & even)
        def _():
            greet(other, lon)

        @pl.when(present & (jnp.logical_not(even) | first_place))
        def _():
            greet(other, west)

        @pl.when(present & wider)
        def _():
            greet(other, east)

    loads = [
        pltpu.make_async_copy(x_hbm, xv, x_sem.at[0]),
        pltpu.make_async_copy(x_hbm.at[:, 0:6], halo.at[0, 3:9, 6:12], x_sem.at[1]),
        pltpu.make_async_copy(x_hbm.at[:, 6:12], halo.at[1, 3:9, 0:6], x_sem.at[2]),
        pltpu.make_async_copy(gain_attn_hbm, gain_attn, w_sem.at[4]),
        pltpu.make_async_copy(w_qkv_hbm, w_qkv, w_sem.at[0]),
        pltpu.make_async_copy(gain_mlp_hbm, gain_mlp, w_sem.at[5]),
        pltpu.make_async_copy(w_out_hbm, w_out, w_sem.at[1]),
        pltpu.make_async_copy(w_up_hbm, w_up, w_sem.at[2]),
        pltpu.make_async_copy(w_down_hbm, w_down, w_sem.at[3]),
    ]
    for load in loads:
        load.start()

    def send(index, src, dst, la, lo):
        return pltpu.make_async_remote_copy(
            src_ref=src,
            dst_ref=dst,
            send_sem=send_sem.at[index],
            recv_sem=recv_sem.at[index],
            device_id={"lat": la, "lon": lo},
            device_id_type=MESH,
        )

    to_east = send(0, x_hbm.at[:, 6:12], halo.at[0, 3:9, 0:6], lat, east)
    to_north = [
        send(1, x_hbm.at[0:3, 0:6], halo.at[0, 9:12, 6:12], north, lon),
        send(2, x_hbm.at[0:3, 6:12], halo.at[0, 9:12, 0:6], north, east),
    ]
    to_south = [
        send(3, x_hbm.at[3:6, 0:6], halo.at[0, 0:3, 6:12], south, lon),
        send(4, x_hbm.at[3:6, 6:12], halo.at[0, 0:3, 0:6], south, east),
    ]
    to_west = send(5, x_hbm.at[:, 0:6], halo.at[1, 3:9, 6:12], lat, west)
    to_north_2 = [
        send(6, x_hbm.at[0:3, 6:12], halo.at[1, 9:12, 0:6], north, lon),
        send(7, x_hbm.at[0:3, 0:6], halo.at[1, 9:12, 6:12], north, west),
    ]
    to_south_2 = [
        send(8, x_hbm.at[3:6, 6:12], halo.at[1, 0:3, 0:6], south, lon),
        send(9, x_hbm.at[3:6, 0:6], halo.at[1, 0:3, 6:12], south, west),
    ]

    ways = ((has_north, far_north, to_north, to_north_2), (has_south, far_south, to_south, to_south_2))

    def straight(far):
        for present, is_far, copies, copies_2 in ways:

            @pl.when(present & (is_far == far) & jnp.logical_not(seven))
            def _():
                copies[0].start()

            @pl.when(present & wider & (is_far == far))
            def _():
                copies_2[0].start()

    def corner(far):
        for present, is_far, copies, copies_2 in ways:

            @pl.when(present & pushes & (is_far == far))
            def _():
                copies_2[1].start()

            @pl.when(present & (is_far == far) & jnp.logical_not(six))
            def _():
                copies[1].start()

    greetings = 1 + ((even & jnp.logical_not(first_place)) | seven).astype(jnp.int32)
    for present, *_ in ways:
        for greets in (even, jnp.logical_not(told), pushes):
            greetings += (present & greets).astype(jnp.int32)
    pl.semaphore_wait(barrier, greetings)

    @pl.when(even)
    def _():
        pl.semaphore_signal(ok_sem.at[0], inc=1, device_id={"lat": lat, "lon": east}, device_id_type=MESH)

        @pl.when(jnp.logical_not(first_place))
        def _():
            pl.semaphore_signal(ok_sem.at[1], inc=1, device_id={"lat": lat, "lon": west}, device_id_type=MESH)

        @pl.when(eight)
        def _():
            to_west.start()

        @pl.when(first_place)
        def _():
            corner(True)

        @pl.when(jnp.logical_not(first_place))
        def _():
            straight(True)

        straight(False)

        @pl.when(jnp.logical_not(six))
        def _():
            to_east.start()

        @pl.when(jnp.logical_not(first_place))
        def _():
            corner(True)

        corner(False)

        @pl.when(first_place)
        def _():
            straight(True)

    @pl.when(last_place)
    def _():
        to_east.start()
        corner(True)
        corner(False)
        pl.semaphore_wait(ok_sem.at[0], 1)
        straight(False)
        straight(True)

    @pl.when(told)
    def _():
        to_east.start()

        @pl.when(seven)
        def _():
            to_west.start()

        pl.semaphore_wait(ok_sem.at[0], 1)

        @pl.when(place == 1)
        def _():
            straight(True)

        straight(False)
        pl.semaphore_wait(ok_sem.at[1], 1)
        corner(True)
        corner(False)

        @pl.when(place != 1)
        def _():
            straight(True)

    key = lax.broadcasted_iota(jnp.int32, (144, 144), 1)
    query = lax.broadcasted_iota(jnp.int32, (144, 144), 0)
    same = lax.rem(key + query, 2) == 0
    for band, known in enumerate(((key >= 72) | has_north, (key >= 72) | has_south)):
        bias[band, 0] = jnp.where(known, 0.0, -1e30)
        bias[band, 1] = jnp.where(known & same, 0.0, -1e30)

    @pl.when(jnp.logical_not(has_north))
    def _():
        halo[:, 0:3] = jnp.zeros((2, 3, 12, 4, D), BF16)

    @pl.when(jnp.logical_not(has_south))
    def _():
        halo[:, 9:12] = jnp.zeros((2, 3, 12, 4, D), BF16)

    def give_back(band):
        return pltpu.make_async_remote_copy(
            src_ref=made.at[0, band, :, 0:6],
            dst_ref=got.at[band],
            send_sem=back_send.at[band],
            recv_sem=back_recv.at[band],
            device_id={"lat": lat, "lon": west},
            device_id_type=MESH,
        )

    def give_on(band):
        return pltpu.make_async_remote_copy(
            src_ref=made.at[1, band, :, 6:12],
            dst_ref=got.at[band],
            send_sem=back_send.at[2 + band],
            recv_sem=back_recv.at[band],
            device_id={"lat": lat, "lon": east},
            device_id_type=MESH,
        )

    for load in loads:
        load.wait()

    low = lax.broadcasted_iota(jnp.int32, (72, 128), 1) < HEAD_DIM
    first = (lat >= middle).astype(jnp.int32)
    only = seven.astype(jnp.int32)

    def project(block):
        normed = norm32(flat(block).astype(F32), gain_attn[...])
        return jnp.concatenate(split_levels(normed), axis=0).astype(BF16)

    def own_rows(window):
        @pl.when(window == 0)
        def _():
            to_east.wait_recv()

        @pl.when(window == 1)
        def _():
            to_west.wait_recv()

        tokens = project(halo[window, 3:9])
        for group in range(2):
            rows = tokens[144 * group : 144 * group + 144]
            for part in range(3):
                own[window, group, part] = dot(rows, w_qkv[:, D * part : D * part + D])

    def step(window, turn):
        band = lax.rem(first + turn, 2)

        @pl.when((turn == 0) & ((window == 0) | seven))
        def _():
            own_rows(window)

        for side, way in ((0, 1), (1, 0)):
            for which in range(2):

                @pl.when((band == side) & ways[side][0] & (window == which))
                def _():
                    for copy in ways[way][2 + which]:
                        copy.wait_recv()

        tokens = project(halo[window, pl.ds(9 * band, 3)])
        others = [dot(tokens, w_qkv[:, D * part : D * part + D]) for part in (1, 2)]
        mixed = []
        for group in range(2):
            rows = slice(72 * group, 72 * group + 72)
            q, k_own, v_own = [own[window, group, part, pl.ds(72 * band, 72)] for part in range(3)]
            q = (q * HEAD_DIM**-0.5).astype(BF16)
            k = jnp.concatenate([others[0][rows], k_own], axis=0).astype(BF16)
            v = jnp.concatenate([others[1][rows], v_own], axis=0).astype(BF16)
            parts = []
            for pair in range(HEADS // 2):
                cols = slice(128 * pair, 128 * pair + 128)
                q_pair = q[:, cols]
                zero = jnp.zeros_like(q_pair)
                stacked = jnp.concatenate([jnp.where(low, q_pair, zero), jnp.where(low, zero, q_pair)], axis=0)
                scores = dot_t(stacked, k[:, cols]) + bias[band, group]
                raised = jnp.exp(scores - jnp.max(scores, axis=-1, keepdims=True))
                total = jnp.sum(raised, axis=-1, keepdims=True)
                out = dot(raised.astype(BF16), v[:, cols]) * (1.0 / total)
                parts.append(jnp.where(low, out[0:72], out[72:144]))
            mixed.append(jnp.concatenate(parts, axis=1))
        made[window, band] = join_levels(*mixed).astype(BF16).reshape(3, 12, 4, D)

        @pl.when((window == 0) & jnp.logical_not(eight))
        def _():
            give_back(band).start()

        @pl.when((window == 1) & six)
        def _():
            give_on(band).start()

    step(only, 0)

    @pl.when(six)
    def _():
        own_rows(1)

    step(only, 1)

    @pl.when(six)
    def _():
        lax.fori_loop(0, 2, lambda turn, carry: (step(1, turn), carry)[1], 0)

    whole = has_whole(lon, n_lon)

    @pl.when(jnp.logical_not(whole))
    def _():
        attended = jnp.concatenate([flat(made[0, band, :, 6:12]) for band in range(2)], axis=0)
        early[...] = feed_forward(attended, flat(xv[:, 0:6]), w_out, gain_mlp, w_up, w_down).reshape(early.shape)

    def sent(condition, copy):
        @pl.when(condition)
        def _():
            copy.wait_send()

    sent(jnp.logical_not(six), to_east)
    sent(pushes, to_west)
    for present, _, copies, copies_2 in ways:
        sent(present & jnp.logical_not(seven), copies[0])
        sent(present & jnp.logical_not(six), copies[1])
        sent(present & wider, copies_2[0])
        sent(present & pushes, copies_2[1])
    for band in range(2):
        sent(jnp.logical_not(pushes | first_place), give_back(band))
        sent(six, give_on(band))

    @pl.when(six)
    def _():
        for band in range(2):
            late[3 * band : 3 * band + 3] = made[1, band, :, 0:6]

    @pl.when(jnp.logical_not(six))
    def _():
        for band in range(2):
            give_back(band).wait_recv()

    @pl.when(jnp.logical_not(six | seven))
    def _():
        for band in range(2):
            late[3 * band : 3 * band + 3] = got[band]

    @pl.when(first_place)
    def _():
        for band in range(2):
            early[3 * band : 3 * band + 3] = made[0, band, :, 6:12]

    @pl.when(seven)
    def _():
        for band in range(2):
            early[3 * band : 3 * band + 3] = got[band]
            late[3 * band : 3 * band + 3] = made[1, band, :, 0:6]

    @pl.when(whole)
    def _():
        attended = jnp.concatenate([flat(early[...]), flat(late[...])], axis=0)
        x = jnp.concatenate([flat(xv[:, 0:6]), flat(xv[:, 6:12])], axis=0)
        values = feed_forward(attended, x, w_out, gain_mlp, w_up, w_down)
        early[...] = values[0:144].reshape(early.shape)
        late[...] = values[144:288].reshape(late.shape)

    for band in range(2):
        sent(first_place, give_back(band))


def solution(mesh):
    n_lat, n_lon = mesh.shape["lat"], mesh.shape["lon"]

    def body(tokens, gain_attn, w_qkv, w_out, gain_mlp, w_up, w_down):
        x = tokens.transpose(1, 2, 0, 3)
        gain_attn, gain_mlp = gain_attn.reshape(1, D), gain_mlp.reshape(1, D)
        hbm = pl.BlockSpec(memory_space=pltpu.HBM)
        vmem = pl.BlockSpec(memory_space=pltpu.VMEM)
        held = [
            pltpu.with_memory_space_constraint(a, pltpu.HBM)
            for a in (x, gain_attn, w_qkv, w_out, gain_mlp, w_up, w_down)
        ]
        half = jax.ShapeDtypeStruct((6, 6, 4, D), BF16)
        passed = [jax.ShapeDtypeStruct(a.shape, a.dtype) for a in (x, w_out, gain_mlp, w_up, w_down)]
        made = pl.pallas_call(
            functools.partial(kernel, n_lat, n_lon),
            out_shape=[half, half] + passed,
            in_specs=[hbm] * 7,
            out_specs=[vmem] * 7,
            scratch_shapes=[
                pltpu.VMEM((1, D), F32),
                pltpu.VMEM((2, 12, 12, 4, D), BF16),
                pltpu.VMEM((2, 2, 3, 12, 4, D), BF16),
                pltpu.VMEM((2, 2, 3, 144, D), F32),
                pltpu.VMEM((2, 3, 6, 4, D), BF16),
                pltpu.VMEM((2, 2, 144, 144), F32),
                pltpu.VMEM((D, 3 * D), BF16),
                pltpu.SemaphoreType.DMA((10,)),
                pltpu.SemaphoreType.DMA((10,)),
                pltpu.SemaphoreType.DMA((4,)),
                pltpu.SemaphoreType.DMA((2,)),
                pltpu.SemaphoreType.DMA((6,)),
                pltpu.SemaphoreType.DMA((3,)),
                pltpu.SemaphoreType.REGULAR((2,)),
            ],
            compiler_params=pltpu.CompilerParams(
                collective_id=0, has_side_effects=True, vmem_limit_bytes=40 * 1024 * 1024
            ),
            cost_estimate=pl.CostEstimate(flops=1_800_000_000, bytes_accessed=7_000_000, transcendentals=1_000_000),
        )(*held)
        out = pl.pallas_call(
            functools.partial(finish, n_lon),
            out_shape=jax.ShapeDtypeStruct(x.shape, BF16),
            in_specs=[vmem] * 7,
            out_specs=hbm,
            scratch_shapes=[pltpu.VMEM((6, 6, 4, D), BF16), pltpu.SemaphoreType.DMA((2,))],
            compiler_params=pltpu.CompilerParams(vmem_limit_bytes=40 * 1024 * 1024),
            cost_estimate=pl.CostEstimate(flops=700_000_000, bytes_accessed=300_000, transcendentals=300_000),
        )(*made)
        return out.transpose(2, 0, 1, 3)

    in_specs = (P(None, "lat", "lon", None), P(), P(), P(), P(), P(), P())
    out_specs = P(None, "lat", "lon", None)
    return jax.shard_map(body, mesh=mesh, in_specs=in_specs, out_specs=out_specs, check_vma=False)
```

```python
import functools

import jax
import jax.numpy as jnp
from jax import lax
from jax.experimental import pallas as pl
from jax.experimental.pallas import tpu as pltpu
from jax.sharding import PartitionSpec as P

HEADS = 8
D = 512
FF = 2048
HEAD_DIM = 64
F32 = jnp.float32
BF16 = jnp.bfloat16
MESH = pl.DeviceIdType.MESH


def norm32(values, gain):
    average = jnp.mean(values, axis=-1, keepdims=True)
    centered = values - average
    spread = jnp.mean(centered * centered, axis=-1, keepdims=True)
    return centered * lax.rsqrt(spread + 1e-05) * gain


def norm(values, gain):
    return norm32(values, gain).astype(BF16)


def inner_levels(shape):
    place = lax.rem(lax.broadcasted_iota(jnp.int32, shape, 1), 4)
    return (place == 1) | (place == 2)


def split_levels(values):
    pairs = values.reshape(values.shape[0] // 16, 2, 8, values.shape[1])
    first, second = pairs[:, 0], pltpu.roll(pairs[:, 1], 2, 1)
    inner = inner_levels(first.shape)
    half = (values.shape[0] // 2, values.shape[1])
    return jnp.where(inner, first, second).reshape(half), jnp.where(inner, second, first).reshape(half)


def join_levels(inner_half, outer_half):
    shape = (inner_half.shape[0] // 8, 8, inner_half.shape[1])
    a, b = inner_half.reshape(shape), outer_half.reshape(shape)
    inner = inner_levels(shape)
    first, second = jnp.where(inner, a, b), pltpu.roll(jnp.where(inner, b, a), 6, 1)
    return jnp.stack([first, second], axis=1).reshape(2 * inner_half.shape[0], inner_half.shape[1])


def flat(block):
    rows = block.shape[0] * block.shape[1] * block.shape[2]
    return block.reshape(rows, block.shape[3])


def gelu(v):
    inner = v * (0.7978845608028654 + 0.035677408136300125 * (v * v))
    return (0.5 * v) * (1.0 + jnp.tanh(inner))


def dot(a, b):
    return jnp.dot(a, b, preferred_element_type=F32)


def dot_t(a, b):
    return lax.dot_general(a, b, (((1,), (1,)), ((), ())), preferred_element_type=F32)


def feed_forward(attended, x, w_out, gain, w_up, w_down):
    residual = (x.astype(F32) + dot(attended, w_out[...])).astype(BF16).astype(F32)
    hidden = gelu(dot(norm(residual, gain[...]), w_up[...])).astype(BF16)
    return (residual + dot(hidden, w_down[...])).astype(BF16)


def has_whole(lon, n_lon):
    place = lax.rem(lon, n_lon // 2)
    return (place == 0) | (place == n_lon // 4 - 1)


def finish(n_lon, early, late, xv, w_out, gain, w_up, w_down, o_hbm, done, sem):
    whole = has_whole(lax.axis_index("lon"), n_lon)
    put = pltpu.make_async_copy(early, o_hbm.at[:, 0:6], sem.at[0])
    put.start()

    def last(src):
        return pltpu.make_async_copy(src, o_hbm.at[:, 6:12], sem.at[1])

    @pl.when(whole)
    def _():
        last(late).start()

    @pl.when(jnp.logical_not(whole))
    def _():
        done[...] = feed_forward(flat(late[...]), flat(xv[:, 6:12]), w_out, gain, w_up, w_down).reshape(done.shape)
        last(done).start()

    put.wait()
    last(done).wait()


def kernel(
    n_lat,
    n_lon,
    x_hbm,
    gain_attn_hbm,
    w_qkv_hbm,
    w_out_hbm,
    gain_mlp_hbm,
    w_up_hbm,
    w_down_hbm,
    early,
    late,
    xv,
    w_out,
    gain_mlp,
    w_up,
    w_down,
    gain_attn,
    halo,
    made,
    own,
    got,
    bias,
    w_qkv,
    send_sem,
    recv_sem,
    back_send,
    back_recv,
    w_sem,
    x_sem,
    ok_sem,
):
    lat = lax.axis_index("lat")
    lon = lax.axis_index("lon")
    west = lax.rem(lon + n_lon - 1, n_lon)
    east = lax.rem(lon + 1, n_lon)
    north = lax.rem(lat + n_lat - 1, n_lat)
    south = lax.rem(lat + 1, n_lat)
    has_north = lat > 0
    has_south = lat < n_lat - 1

    barrier = pltpu.get_barrier_semaphore()

    def greet(la, lo):
        pl.semaphore_signal(barrier, inc=1, device_id={"lat": la, "lon": lo}, device_id_type=MESH)

    middle = n_lat // 2
    far_north, far_south = lat == middle, lat == middle - 1
    even = lax.rem(lon, 2) == 0
    place = lax.rem(lon, n_lon // 2)
    first_place, last_place = place == 0, place == n_lon // 2 - 1
    six, seven, eight = place == n_lon // 4 - 2, place == n_lon // 4 - 1, place == n_lon // 4
    wider, pushes = six | seven, seven | eight
    told = jnp.logical_not(even | last_place)
    greet(lat, west)

    @pl.when(told | six)
    def _():
        greet(lat, east)

    for present, other in ((has_north, north), (has_south, south)):

        @pl.when(present & even)
        def _():
            greet(other, lon)

        @pl.when(present & (jnp.logical_not(even) | first_place))
        def _():
            greet(other, west)

        @pl.when(present & wider)
        def _():
            greet(other, east)

    loads = [
        pltpu.make_async_copy(x_hbm, xv, x_sem.at[0]),
        pltpu.make_async_copy(x_hbm.at[:, 0:6], halo.at[0, 3:9, 6:12], x_sem.at[1]),
        pltpu.make_async_copy(x_hbm.at[:, 6:12], halo.at[1, 3:9, 0:6], x_sem.at[2]),
        pltpu.make_async_copy(gain_attn_hbm, gain_attn, w_sem.at[4]),
        pltpu.make_async_copy(w_qkv_hbm, w_qkv, w_sem.at[0]),
        pltpu.make_async_copy(gain_mlp_hbm, gain_mlp, w_sem.at[5]),
        pltpu.make_async_copy(w_out_hbm, w_out, w_sem.at[1]),
        pltpu.make_async_copy(w_up_hbm, w_up, w_sem.at[2]),
        pltpu.make_async_copy(w_down_hbm, w_down, w_sem.at[3]),
    ]
    for load in loads:
        load.start()

    def send(index, src, dst, la, lo):
        return pltpu.make_async_remote_copy(
            src_ref=src,
            dst_ref=dst,
            send_sem=send_sem.at[index],
            recv_sem=recv_sem.at[index],
            device_id={"lat": la, "lon": lo},
            device_id_type=MESH,
        )

    to_east = send(0, x_hbm.at[:, 6:12], halo.at[0, 3:9, 0:6], lat, east)
    to_north = [
        send(1, x_hbm.at[0:3, 0:6], halo.at[0, 9:12, 6:12], north, lon),
        send(2, x_hbm.at[0:3, 6:12], halo.at[0, 9:12, 0:6], north, east),
    ]
    to_south = [
        send(3, x_hbm.at[3:6, 0:6], halo.at[0, 0:3, 6:12], south, lon),
        send(4, x_hbm.at[3:6, 6:12], halo.at[0, 0:3, 0:6], south, east),
    ]
    to_west = send(5, x_hbm.at[:, 0:6], halo.at[1, 3:9, 6:12], lat, west)
    to_north_2 = [
        send(6, x_hbm.at[0:3, 6:12], halo.at[1, 9:12, 0:6], north, lon),
        send(7, x_hbm.at[0:3, 0:6], halo.at[1, 9:12, 6:12], north, west),
    ]
    to_south_2 = [
        send(8, x_hbm.at[3:6, 6:12], halo.at[1, 0:3, 0:6], south, lon),
        send(9, x_hbm.at[3:6, 0:6], halo.at[1, 0:3, 6:12], south, west),
    ]

    ways = ((has_north, far_north, to_north, to_north_2), (has_south, far_south, to_south, to_south_2))

    def straight(far):
        for present, is_far, copies, copies_2 in ways:

            @pl.when(present & (is_far == far) & jnp.logical_not(seven))
            def _():
                copies[0].start()

            @pl.when(present & wider & (is_far == far))
            def _():
                copies_2[0].start()

    def corner(far):
        for present, is_far, copies, copies_2 in ways:

            @pl.when(present & (seven | (eight & jnp.logical_not(is_far))) & (is_far == far))
            def _():
                copies_2[1].start()

            @pl.when(present & (is_far == far) & jnp.logical_not(six))
            def _():
                copies[1].start()

    greetings = 1 + ((even & jnp.logical_not(first_place)) | seven).astype(jnp.int32)
    for present, *_ in ways:
        for greets in (even, jnp.logical_not(told), pushes):
            greetings += (present & greets).astype(jnp.int32)
    pl.semaphore_wait(barrier, greetings)

    @pl.when(even)
    def _():
        pl.semaphore_signal(ok_sem.at[0], inc=1, device_id={"lat": lat, "lon": east}, device_id_type=MESH)

        @pl.when(jnp.logical_not(first_place))
        def _():
            pl.semaphore_signal(ok_sem.at[1], inc=1, device_id={"lat": lat, "lon": west}, device_id_type=MESH)

        @pl.when(eight)
        def _():
            to_west.start()

        for present, is_far, copies, copies_2 in ways:

            @pl.when(present & eight & is_far)
            def _():
                copies_2[1].start()

        @pl.when(first_place)
        def _():
            corner(True)

        @pl.when(jnp.logical_not(first_place))
        def _():
            straight(True)

        straight(False)

        @pl.when(jnp.logical_not(six))
        def _():
            to_east.start()

        @pl.when(jnp.logical_not(first_place))
        def _():
            corner(True)

        corner(False)

        @pl.when(first_place)
        def _():
            straight(True)

    @pl.when(last_place)
    def _():
        to_east.start()
        corner(True)
        corner(False)
        pl.semaphore_wait(ok_sem.at[0], 1)
        straight(False)
        straight(True)

    @pl.when(told)
    def _():
        to_east.start()

        @pl.when(seven)
        def _():
            to_west.start()

        pl.semaphore_wait(ok_sem.at[0], 1)

        @pl.when(place == 1)
        def _():
            straight(True)

        straight(False)
        pl.semaphore_wait(ok_sem.at[1], 1)
        corner(True)
        corner(False)

        @pl.when(place != 1)
        def _():
            straight(True)

    key = lax.broadcasted_iota(jnp.int32, (144, 144), 1)
    query = lax.broadcasted_iota(jnp.int32, (144, 144), 0)
    same = lax.rem(key + query, 2) == 0
    for band, known in enumerate(((key >= 72) | has_north, (key >= 72) | has_south)):
        bias[band, 0] = jnp.where(known, 0.0, -1e30)
        bias[band, 1] = jnp.where(known & same, 0.0, -1e30)

    @pl.when(jnp.logical_not(has_north))
    def _():
        halo[:, 0:3] = jnp.zeros((2, 3, 12, 4, D), BF16)

    @pl.when(jnp.logical_not(has_south))
    def _():
        halo[:, 9:12] = jnp.zeros((2, 3, 12, 4, D), BF16)

    def give_back(band):
        return pltpu.make_async_remote_copy(
            src_ref=made.at[0, band, :, 0:6],
            dst_ref=got.at[band],
            send_sem=back_send.at[band],
            recv_sem=back_recv.at[band],
            device_id={"lat": lat, "lon": west},
            device_id_type=MESH,
        )

    def give_on(band):
        return pltpu.make_async_remote_copy(
            src_ref=made.at[1, band, :, 6:12],
            dst_ref=got.at[band],
            send_sem=back_send.at[2 + band],
            recv_sem=back_recv.at[band],
            device_id={"lat": lat, "lon": east},
            device_id_type=MESH,
        )

    for load in loads:
        load.wait()

    low = lax.broadcasted_iota(jnp.int32, (72, 128), 1) < HEAD_DIM
    first = (lat >= middle).astype(jnp.int32)
    only = seven.astype(jnp.int32)

    def project(block):
        normed = norm32(flat(block).astype(F32), gain_attn[...])
        return jnp.concatenate(split_levels(normed), axis=0).astype(BF16)

    def own_rows(window):
        @pl.when(window == 0)
        def _():
            to_east.wait_recv()

        @pl.when(window == 1)
        def _():
            to_west.wait_recv()

        tokens = project(halo[window, 3:9])
        for group in range(2):
            rows = tokens[144 * group : 144 * group + 144]
            for part in range(3):
                own[window, group, part] = dot(rows, w_qkv[:, D * part : D * part + D])

    def step(window, turn):
        band = lax.rem(first + turn, 2)

        @pl.when((turn == 0) & ((window == 0) | seven))
        def _():
            own_rows(window)

        for side, way in ((0, 1), (1, 0)):
            for which in range(2):

                @pl.when((band == side) & ways[side][0] & (window == which))
                def _():
                    for copy in ways[way][2 + which]:
                        copy.wait_recv()

        tokens = project(halo[window, pl.ds(9 * band, 3)])
        others = [dot(tokens, w_qkv[:, D * part : D * part + D]) for part in (1, 2)]
        mixed = []
        for group in range(2):
            rows = slice(72 * group, 72 * group + 72)
            q, k_own, v_own = [own[window, group, part, pl.ds(72 * band, 72)] for part in range(3)]
            q = (q * HEAD_DIM**-0.5).astype(BF16)
            k = jnp.concatenate([others[0][rows], k_own], axis=0).astype(BF16)
            v = jnp.concatenate([others[1][rows], v_own], axis=0).astype(BF16)
            parts = []
            for pair in range(HEADS // 2):
                cols = slice(128 * pair, 128 * pair + 128)
                q_pair = q[:, cols]
                zero = jnp.zeros_like(q_pair)
                stacked = jnp.concatenate([jnp.where(low, q_pair, zero), jnp.where(low, zero, q_pair)], axis=0)
                scores = dot_t(stacked, k[:, cols]) + bias[band, group]
                raised = jnp.exp(scores - jnp.max(scores, axis=-1, keepdims=True))
                total = jnp.sum(raised, axis=-1, keepdims=True)
                out = dot(raised.astype(BF16), v[:, cols]) * (1.0 / total)
                parts.append(jnp.where(low, out[0:72], out[72:144]))
            mixed.append(jnp.concatenate(parts, axis=1))
        made[window, band] = join_levels(*mixed).astype(BF16).reshape(3, 12, 4, D)

        @pl.when((window == 0) & jnp.logical_not(eight))
        def _():
            give_back(band).start()

        @pl.when((window == 1) & six)
        def _():
            give_on(band).start()

    step(only, 0)

    @pl.when(six)
    def _():
        own_rows(1)

    step(only, 1)

    @pl.when(six)
    def _():
        lax.fori_loop(0, 2, lambda turn, carry: (step(1, turn), carry)[1], 0)

    whole = has_whole(lon, n_lon)

    @pl.when(jnp.logical_not(whole))
    def _():
        attended = jnp.concatenate([flat(made[0, band, :, 6:12]) for band in range(2)], axis=0)
        early[...] = feed_forward(attended, flat(xv[:, 0:6]), w_out, gain_mlp, w_up, w_down).reshape(early.shape)

    def sent(condition, copy):
        @pl.when(condition)
        def _():
            copy.wait_send()

    sent(jnp.logical_not(six), to_east)
    sent(pushes, to_west)
    for present, _, copies, copies_2 in ways:
        sent(present & jnp.logical_not(seven), copies[0])
        sent(present & jnp.logical_not(six), copies[1])
        sent(present & wider, copies_2[0])
        sent(present & pushes, copies_2[1])
    for band in range(2):
        sent(jnp.logical_not(pushes | first_place), give_back(band))
        sent(six, give_on(band))

    @pl.when(six)
    def _():
        for band in range(2):
            late[3 * band : 3 * band + 3] = made[1, band, :, 0:6]

    @pl.when(jnp.logical_not(six))
    def _():
        for band in range(2):
            give_back(band).wait_recv()

    @pl.when(jnp.logical_not(six | seven))
    def _():
        for band in range(2):
            late[3 * band : 3 * band + 3] = got[band]

    @pl.when(first_place)
    def _():
        for band in range(2):
            early[3 * band : 3 * band + 3] = made[0, band, :, 6:12]

    @pl.when(seven)
    def _():
        for band in range(2):
            early[3 * band : 3 * band + 3] = got[band]
            late[3 * band : 3 * band + 3] = made[1, band, :, 0:6]

    @pl.when(whole)
    def _():
        attended = jnp.concatenate([flat(early[...]), flat(late[...])], axis=0)
        x = jnp.concatenate([flat(xv[:, 0:6]), flat(xv[:, 6:12])], axis=0)
        values = feed_forward(attended, x, w_out, gain_mlp, w_up, w_down)
        early[...] = values[0:144].reshape(early.shape)
        late[...] = values[144:288].reshape(late.shape)

    for band in range(2):
        sent(first_place, give_back(band))


def solution(mesh):
    n_lat, n_lon = mesh.shape["lat"], mesh.shape["lon"]

    def body(tokens, gain_attn, w_qkv, w_out, gain_mlp, w_up, w_down):
        x = tokens.transpose(1, 2, 0, 3)
        gain_attn, gain_mlp = gain_attn.reshape(1, D), gain_mlp.reshape(1, D)
        hbm = pl.BlockSpec(memory_space=pltpu.HBM)
        vmem = pl.BlockSpec(memory_space=pltpu.VMEM)
        held = [
            pltpu.with_memory_space_constraint(a, pltpu.HBM)
            for a in (x, gain_attn, w_qkv, w_out, gain_mlp, w_up, w_down)
        ]
        half = jax.ShapeDtypeStruct((6, 6, 4, D), BF16)
        passed = [jax.ShapeDtypeStruct(a.shape, a.dtype) for a in (x, w_out, gain_mlp, w_up, w_down)]
        made = pl.pallas_call(
            functools.partial(kernel, n_lat, n_lon),
            out_shape=[half, half] + passed,
            in_specs=[hbm] * 7,
            out_specs=[vmem] * 7,
            scratch_shapes=[
                pltpu.VMEM((1, D), F32),
                pltpu.VMEM((2, 12, 12, 4, D), BF16),
                pltpu.VMEM((2, 2, 3, 12, 4, D), BF16),
                pltpu.VMEM((2, 2, 3, 144, D), F32),
                pltpu.VMEM((2, 3, 6, 4, D), BF16),
                pltpu.VMEM((2, 2, 144, 144), F32),
                pltpu.VMEM((D, 3 * D), BF16),
                pltpu.SemaphoreType.DMA((10,)),
                pltpu.SemaphoreType.DMA((10,)),
                pltpu.SemaphoreType.DMA((4,)),
                pltpu.SemaphoreType.DMA((2,)),
                pltpu.SemaphoreType.DMA((6,)),
                pltpu.SemaphoreType.DMA((3,)),
                pltpu.SemaphoreType.REGULAR((2,)),
            ],
            compiler_params=pltpu.CompilerParams(
                collective_id=0, has_side_effects=True, vmem_limit_bytes=40 * 1024 * 1024
            ),
            cost_estimate=pl.CostEstimate(flops=1_800_000_000, bytes_accessed=7_000_000, transcendentals=1_000_000),
        )(*held)
        out = pl.pallas_call(
            functools.partial(finish, n_lon),
            out_shape=jax.ShapeDtypeStruct(x.shape, BF16),
            in_specs=[vmem] * 7,
            out_specs=hbm,
            scratch_shapes=[pltpu.VMEM((6, 6, 4, D), BF16), pltpu.SemaphoreType.DMA((2,))],
            compiler_params=pltpu.CompilerParams(vmem_limit_bytes=40 * 1024 * 1024),
            cost_estimate=pl.CostEstimate(flops=700_000_000, bytes_accessed=300_000, transcendentals=300_000),
        )(*made)
        return out.transpose(2, 0, 1, 3)

    in_specs = (P(None, "lat", "lon", None), P(), P(), P(), P(), P(), P())
    out_specs = P(None, "lat", "lon", None)
    return jax.shard_map(body, mesh=mesh, in_specs=in_specs, out_specs=out_specs, check_vma=False)
```

```python
import functools

import jax
import jax.numpy as jnp
from jax import lax
from jax.experimental import pallas as pl
from jax.experimental.pallas import tpu as pltpu
from jax.sharding import PartitionSpec as P

HEADS = 8
D = 512
FF = 2048
HEAD_DIM = 64
F32 = jnp.float32
BF16 = jnp.bfloat16
MESH = pl.DeviceIdType.MESH


def norm32(values, gain):
    average = jnp.mean(values, axis=-1, keepdims=True)
    centered = values - average
    spread = jnp.mean(centered * centered, axis=-1, keepdims=True)
    return centered * lax.rsqrt(spread + 1e-05) * gain


def norm(values, gain):
    return norm32(values, gain).astype(BF16)


def inner_levels(shape):
    place = lax.rem(lax.broadcasted_iota(jnp.int32, shape, 1), 4)
    return (place == 1) | (place == 2)


def split_levels(values):
    pairs = values.reshape(values.shape[0] // 16, 2, 8, values.shape[1])
    first, second = pairs[:, 0], pltpu.roll(pairs[:, 1], 2, 1)
    inner = inner_levels(first.shape)
    half = (values.shape[0] // 2, values.shape[1])
    return jnp.where(inner, first, second).reshape(half), jnp.where(inner, second, first).reshape(half)


def join_levels(inner_half, outer_half):
    shape = (inner_half.shape[0] // 8, 8, inner_half.shape[1])
    a, b = inner_half.reshape(shape), outer_half.reshape(shape)
    inner = inner_levels(shape)
    first, second = jnp.where(inner, a, b), pltpu.roll(jnp.where(inner, b, a), 6, 1)
    return jnp.stack([first, second], axis=1).reshape(2 * inner_half.shape[0], inner_half.shape[1])


def flat(block):
    rows = block.shape[0] * block.shape[1] * block.shape[2]
    return block.reshape(rows, block.shape[3])


def gelu(v):
    inner = v * (0.7978845608028654 + 0.035677408136300125 * (v * v))
    return (0.5 * v) * (1.0 + jnp.tanh(inner))


def dot(a, b):
    return jnp.dot(a, b, preferred_element_type=F32)


def dot_t(a, b):
    return lax.dot_general(a, b, (((1,), (1,)), ((), ())), preferred_element_type=F32)


def feed_forward(attended, x, w_out, gain, w_up, w_down):
    residual = (x.astype(F32) + dot(attended, w_out[...])).astype(BF16).astype(F32)
    hidden = gelu(dot(norm(residual, gain[...]), w_up[...])).astype(BF16)
    return (residual + dot(hidden, w_down[...])).astype(BF16)


def has_whole(lon, n_lon):
    place = lax.rem(lon, n_lon // 2)
    return (place == 0) | (place == n_lon // 4 - 1)


def finish(n_lon, early, late, xv, w_out, gain, w_up, w_down, o_hbm, done, sem):
    whole = has_whole(lax.axis_index("lon"), n_lon)
    put = pltpu.make_async_copy(early, o_hbm.at[:, 0:6], sem.at[0])
    put.start()

    def last(src):
        return pltpu.make_async_copy(src, o_hbm.at[:, 6:12], sem.at[1])

    @pl.when(whole)
    def _():
        last(late).start()

    @pl.when(jnp.logical_not(whole))
    def _():
        done[...] = feed_forward(flat(late[...]), flat(xv[:, 6:12]), w_out, gain, w_up, w_down).reshape(done.shape)
        last(done).start()

    put.wait()
    last(done).wait()


def kernel(
    n_lat,
    n_lon,
    x_hbm,
    gain_attn_hbm,
    w_qkv_hbm,
    w_out_hbm,
    gain_mlp_hbm,
    w_up_hbm,
    w_down_hbm,
    early,
    late,
    xv,
    w_out,
    gain_mlp,
    w_up,
    w_down,
    gain_attn,
    halo,
    made,
    own,
    got,
    bias,
    w_qkv,
    send_sem,
    recv_sem,
    back_send,
    back_recv,
    w_sem,
    x_sem,
    ok_sem,
):
    lat = lax.axis_index("lat")
    lon = lax.axis_index("lon")
    west = lax.rem(lon + n_lon - 1, n_lon)
    east = lax.rem(lon + 1, n_lon)
    north = lax.rem(lat + n_lat - 1, n_lat)
    south = lax.rem(lat + 1, n_lat)
    has_north = lat > 0
    has_south = lat < n_lat - 1

    barrier = pltpu.get_barrier_semaphore()

    def greet(la, lo):
        pl.semaphore_signal(barrier, inc=1, device_id={"lat": la, "lon": lo}, device_id_type=MESH)

    middle = n_lat // 2
    far_north, far_south = lat == middle, lat == middle - 1
    even = lax.rem(lon, 2) == 0
    place = lax.rem(lon, n_lon // 2)
    first_place, last_place = place == 0, place == n_lon // 2 - 1
    six, seven, eight = place == n_lon // 4 - 2, place == n_lon // 4 - 1, place == n_lon // 4
    wider, pushes = six | seven, seven | eight
    told = jnp.logical_not(even | last_place)
    greet(lat, west)

    @pl.when(told | six)
    def _():
        greet(lat, east)

    for present, other in ((has_north, north), (has_south, south)):

        @pl.when(present & even)
        def _():
            greet(other, lon)

        @pl.when(present & (jnp.logical_not(even) | first_place))
        def _():
            greet(other, west)

        @pl.when(present & wider)
        def _():
            greet(other, east)

    loads = [
        pltpu.make_async_copy(x_hbm, xv, x_sem.at[0]),
        pltpu.make_async_copy(x_hbm.at[:, 0:6], halo.at[0, 3:9, 6:12], x_sem.at[1]),
        pltpu.make_async_copy(x_hbm.at[:, 6:12], halo.at[1, 3:9, 0:6], x_sem.at[2]),
        pltpu.make_async_copy(gain_attn_hbm, gain_attn, w_sem.at[4]),
        pltpu.make_async_copy(w_qkv_hbm, w_qkv, w_sem.at[0]),
        pltpu.make_async_copy(gain_mlp_hbm, gain_mlp, w_sem.at[5]),
        pltpu.make_async_copy(w_out_hbm, w_out, w_sem.at[1]),
        pltpu.make_async_copy(w_up_hbm, w_up, w_sem.at[2]),
        pltpu.make_async_copy(w_down_hbm, w_down, w_sem.at[3]),
    ]
    for load in loads:
        load.start()

    def send(index, src, dst, la, lo):
        return pltpu.make_async_remote_copy(
            src_ref=src,
            dst_ref=dst,
            send_sem=send_sem.at[index],
            recv_sem=recv_sem.at[index],
            device_id={"lat": la, "lon": lo},
            device_id_type=MESH,
        )

    to_east = send(0, x_hbm.at[:, 6:12], halo.at[0, 3:9, 0:6], lat, east)
    to_north = [
        send(1, x_hbm.at[0:3, 0:6], halo.at[0, 9:12, 6:12], north, lon),
        send(2, x_hbm.at[0:3, 6:12], halo.at[0, 9:12, 0:6], north, east),
    ]
    to_south = [
        send(3, x_hbm.at[3:6, 0:6], halo.at[0, 0:3, 6:12], south, lon),
        send(4, x_hbm.at[3:6, 6:12], halo.at[0, 0:3, 0:6], south, east),
    ]
    to_west = send(5, x_hbm.at[:, 0:6], halo.at[1, 3:9, 6:12], lat, west)
    to_north_2 = [
        send(6, x_hbm.at[0:3, 6:12], halo.at[1, 9:12, 0:6], north, lon),
        send(7, x_hbm.at[0:3, 0:6], halo.at[1, 9:12, 6:12], north, west),
    ]
    to_south_2 = [
        send(8, x_hbm.at[3:6, 6:12], halo.at[1, 0:3, 0:6], south, lon),
        send(9, x_hbm.at[3:6, 0:6], halo.at[1, 0:3, 6:12], south, west),
    ]

    ways = ((has_north, far_north, to_north, to_north_2), (has_south, far_south, to_south, to_south_2))

    def straight(far):
        for present, is_far, copies, copies_2 in ways:

            @pl.when(present & (is_far == far) & jnp.logical_not(seven))
            def _():
                copies[0].start()

            @pl.when(present & wider & (is_far == far))
            def _():
                copies_2[0].start()

    def corner(far):
        for present, is_far, copies, copies_2 in ways:

            @pl.when(present & pushes & (is_far == far))
            def _():
                copies_2[1].start()

            @pl.when(present & (is_far == far) & jnp.logical_not(six))
            def _():
                copies[1].start()

    greetings = 1 + ((even & jnp.logical_not(first_place)) | seven).astype(jnp.int32)
    for present, *_ in ways:
        for greets in (even, jnp.logical_not(told), pushes):
            greetings += (present & greets).astype(jnp.int32)
    pl.semaphore_wait(barrier, greetings)

    @pl.when(even)
    def _():
        pl.semaphore_signal(ok_sem.at[0], inc=1, device_id={"lat": lat, "lon": east}, device_id_type=MESH)

        @pl.when(jnp.logical_not(first_place))
        def _():
            pl.semaphore_signal(ok_sem.at[1], inc=1, device_id={"lat": lat, "lon": west}, device_id_type=MESH)

        @pl.when(eight)
        def _():
            to_west.start()

        @pl.when(first_place)
        def _():
            corner(True)

        @pl.when(jnp.logical_not(first_place))
        def _():
            straight(True)

        straight(False)

        @pl.when(jnp.logical_not(six))
        def _():
            to_east.start()

        @pl.when(jnp.logical_not(first_place))
        def _():
            corner(True)

        corner(False)

        @pl.when(first_place)
        def _():
            straight(True)

    @pl.when(last_place)
    def _():
        to_east.start()
        corner(True)
        corner(False)
        pl.semaphore_wait(ok_sem.at[0], 1)
        straight(False)
        straight(True)

    @pl.when(told)
    def _():
        to_east.start()

        @pl.when(seven)
        def _():
            to_west.start()

        pl.semaphore_wait(ok_sem.at[0], 1)

        @pl.when(place == 1)
        def _():
            straight(True)

        straight(False)
        pl.semaphore_wait(ok_sem.at[1], 1)
        corner(True)
        corner(False)

        @pl.when(place != 1)
        def _():
            straight(True)

    key = lax.broadcasted_iota(jnp.int32, (144, 144), 1)
    query = lax.broadcasted_iota(jnp.int32, (144, 144), 0)
    same = lax.rem(key + query, 2) == 0
    for band, known in enumerate(((key >= 72) | has_north, (key >= 72) | has_south)):
        bias[band, 0] = jnp.where(known, 0.0, -1e30)
        bias[band, 1] = jnp.where(known & same, 0.0, -1e30)

    @pl.when(jnp.logical_not(has_north))
    def _():
        halo[:, 0:3] = jnp.zeros((2, 3, 12, 4, D), BF16)

    @pl.when(jnp.logical_not(has_south))
    def _():
        halo[:, 9:12] = jnp.zeros((2, 3, 12, 4, D), BF16)

    def give_back(band):
        return pltpu.make_async_remote_copy(
            src_ref=made.at[0, band, :, 0:6],
            dst_ref=got.at[band],
            send_sem=back_send.at[band],
            recv_sem=back_recv.at[band],
            device_id={"lat": lat, "lon": west},
            device_id_type=MESH,
        )

    def give_on(band):
        return pltpu.make_async_remote_copy(
            src_ref=made.at[1, band, :, 6:12],
            dst_ref=got.at[band],
            send_sem=back_send.at[2 + band],
            recv_sem=back_recv.at[band],
            device_id={"lat": lat, "lon": east},
            device_id_type=MESH,
        )

    for load in loads:
        load.wait()

    low = lax.broadcasted_iota(jnp.int32, (72, 128), 1) < HEAD_DIM
    first = (lat >= middle).astype(jnp.int32)
    only = seven.astype(jnp.int32)

    def project(block):
        normed = norm32(flat(block).astype(F32), gain_attn[...])
        return jnp.concatenate(split_levels(normed), axis=0).astype(BF16)

    def own_rows(window):
        @pl.when(window == 0)
        def _():
            to_east.wait_recv()

        @pl.when(window == 1)
        def _():
            to_west.wait_recv()

        tokens = project(halo[window, 3:9])
        for group in range(2):
            rows = tokens[144 * group : 144 * group + 144]
            for part in range(3):
                scale = HEAD_DIM**-0.5 if part == 0 else 1.0
                own[window, group, part] = dot(rows, w_qkv[:, D * part : D * part + D]) * scale

    def step(window, turn):
        band = lax.rem(first + turn, 2)

        @pl.when((turn == 0) & ((window == 0) | seven))
        def _():
            own_rows(window)

        for side, way in ((0, 1), (1, 0)):
            for which in range(2):

                @pl.when((band == side) & ways[side][0] & (window == which))
                def _():
                    for copy in ways[way][2 + which]:
                        copy.wait_recv()

        tokens = project(halo[window, pl.ds(9 * band, 3)])
        others = [dot(tokens, w_qkv[:, D * part : D * part + D]) for part in (1, 2)]
        mixed = []
        for group in range(2):
            rows = slice(72 * group, 72 * group + 72)
            q, k_own, v_own = [own[window, group, part, pl.ds(72 * band, 72)] for part in range(3)]
            q = q.astype(BF16)
            k = jnp.concatenate([others[0][rows], k_own], axis=0).astype(BF16)
            v = jnp.concatenate([others[1][rows], v_own], axis=0).astype(BF16)
            parts = []
            for pair in range(HEADS // 2):
                cols = slice(128 * pair, 128 * pair + 128)
                q_pair = q[:, cols]
                zero = jnp.zeros_like(q_pair)
                stacked = jnp.concatenate([jnp.where(low, q_pair, zero), jnp.where(low, zero, q_pair)], axis=0)
                scores = dot_t(stacked, k[:, cols]) + bias[band, group]
                raised = jnp.exp(scores - jnp.max(scores, axis=-1, keepdims=True))
                total = jnp.sum(raised, axis=-1, keepdims=True)
                out = dot(raised.astype(BF16), v[:, cols]) * (1.0 / total)
                parts.append(jnp.where(low, out[0:72], out[72:144]))
            mixed.append(jnp.concatenate(parts, axis=1))
        made[window, band] = join_levels(*mixed).astype(BF16).reshape(3, 12, 4, D)

        @pl.when((window == 0) & jnp.logical_not(eight))
        def _():
            give_back(band).start()

        @pl.when((window == 1) & six)
        def _():
            give_on(band).start()

    step(only, 0)

    @pl.when(six)
    def _():
        own_rows(1)

    step(only, 1)

    @pl.when(six)
    def _():
        lax.fori_loop(0, 2, lambda turn, carry: (step(1, turn), carry)[1], 0)

    whole = has_whole(lon, n_lon)

    @pl.when(jnp.logical_not(whole))
    def _():
        attended = jnp.concatenate([flat(made[0, band, :, 6:12]) for band in range(2)], axis=0)
        early[...] = feed_forward(attended, flat(xv[:, 0:6]), w_out, gain_mlp, w_up, w_down).reshape(early.shape)

    def sent(condition, copy):
        @pl.when(condition)
        def _():
            copy.wait_send()

    sent(jnp.logical_not(six), to_east)
    sent(pushes, to_west)
    for present, _, copies, copies_2 in ways:
        sent(present & jnp.logical_not(seven), copies[0])
        sent(present & jnp.logical_not(six), copies[1])
        sent(present & wider, copies_2[0])
        sent(present & pushes, copies_2[1])
    for band in range(2):
        sent(jnp.logical_not(pushes | first_place), give_back(band))
        sent(six, give_on(band))

    @pl.when(six)
    def _():
        for band in range(2):
            late[3 * band : 3 * band + 3] = made[1, band, :, 0:6]

    @pl.when(jnp.logical_not(six))
    def _():
        for band in range(2):
            give_back(band).wait_recv()

    @pl.when(jnp.logical_not(six | seven))
    def _():
        for band in range(2):
            late[3 * band : 3 * band + 3] = got[band]

    @pl.when(first_place)
    def _():
        for band in range(2):
            early[3 * band : 3 * band + 3] = made[0, band, :, 6:12]

    @pl.when(seven)
    def _():
        for band in range(2):
            early[3 * band : 3 * band + 3] = got[band]
            late[3 * band : 3 * band + 3] = made[1, band, :, 0:6]

    @pl.when(whole)
    def _():
        attended = jnp.concatenate([flat(early[...]), flat(late[...])], axis=0)
        x = jnp.concatenate([flat(xv[:, 0:6]), flat(xv[:, 6:12])], axis=0)
        values = feed_forward(attended, x, w_out, gain_mlp, w_up, w_down)
        early[...] = values[0:144].reshape(early.shape)
        late[...] = values[144:288].reshape(late.shape)

    for band in range(2):
        sent(first_place, give_back(band))


def solution(mesh):
    n_lat, n_lon = mesh.shape["lat"], mesh.shape["lon"]

    def body(tokens, gain_attn, w_qkv, w_out, gain_mlp, w_up, w_down):
        x = tokens.transpose(1, 2, 0, 3)
        gain_attn, gain_mlp = gain_attn.reshape(1, D), gain_mlp.reshape(1, D)
        hbm = pl.BlockSpec(memory_space=pltpu.HBM)
        vmem = pl.BlockSpec(memory_space=pltpu.VMEM)
        held = [
            pltpu.with_memory_space_constraint(a, pltpu.HBM)
            for a in (x, gain_attn, w_qkv, w_out, gain_mlp, w_up, w_down)
        ]
        half = jax.ShapeDtypeStruct((6, 6, 4, D), BF16)
        passed = [jax.ShapeDtypeStruct(a.shape, a.dtype) for a in (x, w_out, gain_mlp, w_up, w_down)]
        made = pl.pallas_call(
            functools.partial(kernel, n_lat, n_lon),
            out_shape=[half, half] + passed,
            in_specs=[hbm] * 7,
            out_specs=[vmem] * 7,
            scratch_shapes=[
                pltpu.VMEM((1, D), F32),
                pltpu.VMEM((2, 12, 12, 4, D), BF16),
                pltpu.VMEM((2, 2, 3, 12, 4, D), BF16),
                pltpu.VMEM((2, 2, 3, 144, D), F32),
                pltpu.VMEM((2, 3, 6, 4, D), BF16),
                pltpu.VMEM((2, 2, 144, 144), F32),
                pltpu.VMEM((D, 3 * D), BF16),
                pltpu.SemaphoreType.DMA((10,)),
                pltpu.SemaphoreType.DMA((10,)),
                pltpu.SemaphoreType.DMA((4,)),
                pltpu.SemaphoreType.DMA((2,)),
                pltpu.SemaphoreType.DMA((6,)),
                pltpu.SemaphoreType.DMA((3,)),
                pltpu.SemaphoreType.REGULAR((2,)),
            ],
            compiler_params=pltpu.CompilerParams(
                collective_id=0, has_side_effects=True, vmem_limit_bytes=40 * 1024 * 1024
            ),
            cost_estimate=pl.CostEstimate(flops=1_800_000_000, bytes_accessed=7_000_000, transcendentals=1_000_000),
        )(*held)
        out = pl.pallas_call(
            functools.partial(finish, n_lon),
            out_shape=jax.ShapeDtypeStruct(x.shape, BF16),
            in_specs=[vmem] * 7,
            out_specs=hbm,
            scratch_shapes=[pltpu.VMEM((6, 6, 4, D), BF16), pltpu.SemaphoreType.DMA((2,))],
            compiler_params=pltpu.CompilerParams(vmem_limit_bytes=40 * 1024 * 1024),
            cost_estimate=pl.CostEstimate(flops=700_000_000, bytes_accessed=300_000, transcendentals=300_000),
        )(*made)
        return out.transpose(2, 0, 1, 3)

    in_specs = (P(None, "lat", "lon", None), P(), P(), P(), P(), P(), P())
    out_specs = P(None, "lat", "lon", None)
    return jax.shard_map(body, mesh=mesh, in_specs=in_specs, out_specs=out_specs, check_vma=False)
```
